256 devices in a mesh: scan: 64 (over x, y, z_lo, core), tile: 4 (over z_hi).
Axes of the slice: x: 4, y: 4, z: 8 (z_hi: 4, z_lo: 2; z = z_hi * 2 + z_lo), core: 2. Of those that a mesh axis runs over, the one named last changes fastest.
Arguments:
- object_field: float32 [2, 16384, 1024], P(None, 'scan', 'tile'), may hold values from -4.2 to 4.2
- probe_modes: float32 [8, 2, 256, 256], P('tile'), may hold values from -2.1 to 2.1
- amplitudes: bfloat16 [512, 256, 256], P('scan'), may hold values from 0.25 to 3
- positions: int32 [512, 2], P('scan'), may hold values from 0 to 16128, as said below
- counts: int32 [64], P('scan'), may hold values from 1 to 8, as said below
Outputs:
- new_object: float32 [2, 16384, 1024], P(None, 'scan', 'tile')
- probe_step: float32 [8, 2, 256, 256], P('tile')
The draws below stay inside these ranges and needn't reach their ends.
Inputs may be any that keep to these rules, and one draw needn't show every extreme that they name: `positions`: slot j's row offset lies in rows (j // 8) * 256 to (j // 8) * 256 + 255; every window lies inside the object: row offsets at most 16128, column offsets at most 768. `counts`: some scan index holds 8 live slots and some holds one.
All inputs are finite; a program needn't handle non-finite values.
Results may differ from the reference program's by a relative error of at most 0.003.
Values may be sent and summed in bfloat16 or wider, within the bound.
A program may use at most 128 MiB of HBM per device.

```python
import math
import jax
import jax.numpy as jnp
from jax import lax

W = 256
MODES = 8
SLOTS = 8
TR = 256
NOR = 16384
NOC = 1024
NPAT = 512
N_SCAN = 64


def draw_positions(key, part):
    first_key, second_key = jax.random.split(jax.random.fold_in(key, 11), 2)
    slot_ids = jnp.arange(NPAT, dtype=jnp.int32)
    band_start = slot_ids // SLOTS * TR
    row_offsets = band_start + jax.random.randint(first_key, (NPAT,), 0, TR, dtype=jnp.int32)
    row_offsets = jnp.minimum(row_offsets, NOR - W)
    row_offsets = row_offsets.at[0].set(0).at[NPAT - 1].set(NOR - W)
    col_offsets = jax.random.randint(second_key, (NPAT,), 0, NOC - W + 1, dtype=jnp.int32)
    col_offsets = col_offsets.at[0].set(0).at[1].set(NOC - W)
    return jnp.stack([row_offsets, col_offsets], axis=1).astype(jnp.int32)


def draw_counts(key, part):
    first_key, second_key, third_key = jax.random.split(jax.random.fold_in(key, 23), 3)
    values = jax.random.randint(first_key, (N_SCAN,), 1, SLOTS + 1, dtype=jnp.int32)
    full_index = jax.random.randint(second_key, (), 0, N_SCAN, dtype=jnp.int32)
    single_index = (full_index + 1 + jax.random.randint(third_key, (), 0, N_SCAN - 1, dtype=jnp.int32)) % N_SCAN
    values = values.at[full_index].set(SLOTS).at[single_index].set(1)
    return values.astype(jnp.int32)


def block_levels(rng, extent, cuts, smallest, top_value):
    level = 1.0
    for dim, blocks in cuts:
        steps = jax.random.uniform(jax.random.fold_in(jax.random.fold_in(rng, 6), dim), (blocks,), jnp.float32, smallest / len(cuts), top_value / len(cuts))
        level = level * jnp.repeat(jnp.exp(steps), extent[dim] // blocks).reshape((-1,) + (1,) * (len(extent) - 1 - dim))
    return level


def normal_values(stream_key, dims, spread, limit, pieces=(), kind=jnp.bfloat16):
    loudness = block_levels(stream_key, dims, pieces, -0.22, 0.18) if pieces else 1.0
    entries = jax.random.normal(stream_key, dims, jnp.float32) * spread * loudness
    return jnp.minimum(jnp.maximum(entries, -limit), limit).astype(kind)


def setup_inputs(seed: int = 0) -> dict:
    key_list = jax.random.split(jax.random.key(seed), 6)
    object_field = normal_values(key_list[0], (2, NOR, NOC), 0.7, 4.2, ((1, 64), (2, 4)), jnp.float32)
    probe_modes = normal_values(key_list[1], (MODES, 2, W, W), 0.35, 2.1, ((0, 4),), jnp.float32)
    amplitudes = jnp.clip(0.25 + 2.75 * jax.random.uniform(key_list[2], (NPAT, W, W), jnp.float32) ** block_levels(key_list[2], (NPAT, W, W), ((0, 64),), -0.2, 0.2), 0.25, 3.0).astype(jnp.bfloat16)
    positions = draw_positions(jax.random.fold_in(key_list[5], 71), 0)
    counts = draw_counts(jax.random.fold_in(key_list[5], 71), 0)
    return dict(object_field=object_field, probe_modes=probe_modes, amplitudes=amplitudes, positions=positions, counts=counts)


damping = 1.0
amp_floor = 0.5

def dft_tables(win_width):
    index_row = jnp.arange(win_width, dtype=jnp.int32)
    products = index_row[:, None] * index_row[None, :] % win_width
    phase_angle = products.astype(jnp.float32) * (2.0 * math.pi / win_width)
    norm_scale = 1.0 / math.sqrt(win_width)
    real_part = (jnp.cos(phase_angle) * norm_scale).astype(jnp.bfloat16)
    imag_part = (-jnp.sin(phase_angle) * norm_scale).astype(jnp.bfloat16)
    return (real_part, imag_part)

def transform(rowform, right_table, left_table, win_width):
    half_done = jnp.einsum('...ak,kl->...al', rowform.astype(jnp.float32), right_table.astype(jnp.float32), precision=lax.Precision.HIGHEST).astype(jnp.bfloat16)
    full_block = jnp.einsum('ca,...ak->...ck', left_table.astype(jnp.float32), half_done.astype(jnp.float32), precision=lax.Precision.HIGHEST)
    real_out = full_block[..., :win_width, :win_width] - full_block[..., win_width:, win_width:]
    imag_out = full_block[..., :win_width, win_width:] + full_block[..., win_width:, :win_width]
    return (real_out, imag_out)

def reference(object_field, probe_modes, amplitudes, positions, counts):
    real_part, imag_part = dft_tables(W)
    right_fwd = jnp.block([[real_part, imag_part], [-imag_part, real_part]])
    left_fwd = jnp.concatenate([real_part, imag_part], axis=0)
    right_inv = jnp.block([[real_part, -imag_part], [imag_part, real_part]])
    left_inv = jnp.concatenate([real_part, -imag_part], axis=0)
    object_low = object_field.astype(jnp.bfloat16)
    probe_re = probe_modes[:, 0]
    probe_im = probe_modes[:, 1]
    probe_power = lax.optimization_barrier(jnp.sum(probe_re * probe_re + probe_im * probe_im, axis=0))
    zero_index = jnp.zeros((), jnp.int32)

    def accumulate(running, inputs):
        buffer, grad_sum, weight_sum = running
        slot_index, place, amplitude = inputs
        row_at = place[0]
        col_at = place[1]
        window = lax.dynamic_slice(object_low, (zero_index, row_at, col_at), (2, W, W))
        live = (slot_index % SLOTS < counts[slot_index // SLOTS]).astype(jnp.float32)
        window_re = window[0].astype(jnp.float32)
        window_im = window[1].astype(jnp.float32)
        exit_wave = jnp.concatenate([probe_re * window_re - probe_im * window_im, probe_re * window_im + probe_im * window_re], axis=-1).astype(jnp.bfloat16)
        far_re, far_im = transform(exit_wave, right_fwd, left_fwd, W)
        intensity = lax.optimization_barrier(jnp.sum(far_re * far_re + far_im * far_im, axis=0))
        factor = live * (amplitude.astype(jnp.float32) / jnp.maximum(jnp.sqrt(intensity), amp_floor) - 1.0)
        change = jnp.concatenate([factor * far_re, factor * far_im], axis=-1).astype(jnp.bfloat16)
        near_re, near_im = transform(change, right_inv, left_inv, W)
        numer = jnp.stack([lax.optimization_barrier(jnp.sum(probe_re * near_re + probe_im * near_im, axis=0)), lax.optimization_barrier(jnp.sum(probe_re * near_im - probe_im * near_re, axis=0)), live * probe_power])
        grads = jnp.stack([window_re * near_re + window_im * near_im, window_re * near_im - window_im * near_re], axis=1)
        weight = window_re * window_re + window_im * window_im
        region = lax.dynamic_slice(buffer, (zero_index, row_at, col_at), (3, W, W))
        buffer = lax.dynamic_update_slice(buffer, region + numer, (zero_index, row_at, col_at))
        return ((buffer, grad_sum + grads, weight_sum + live * weight), None)
    init = (jnp.zeros((3, NOR, NOC), jnp.float32), jnp.zeros((MODES, 2, W, W), jnp.float32), jnp.zeros((W, W), jnp.float32))
    slot_ids = jnp.arange(NPAT, dtype=jnp.int32)
    (buffer, grad_sum, weight_sum), _ = lax.scan(accumulate, init, (slot_ids, positions, amplitudes))
    new_object = object_field + buffer[0:2] / (buffer[2] + damping)[None]
    probe_step = grad_sum / (weight_sum + damping)[None, None]
    return (new_object, probe_step)
```

```python
import functools
import math

import jax
import jax.numpy as jnp
import numpy as np
from jax import lax
from jax.experimental import pallas as pl
from jax.experimental.pallas import tpu as pltpu
from jax.sharding import PartitionSpec as P

damping = 1.0
amp_floor = 0.5
MESH = pl.DeviceIdType.MESH
BF = jnp.bfloat16
F32 = jnp.float32


def dft_tables(width):
    index = np.arange(width)
    angle = (index[:, None] * index[None, :] % width) * (2.0 * math.pi / width)
    scale = 1.0 / math.sqrt(width)
    return (np.cos(angle) * scale).astype(BF), (-np.sin(angle) * scale).astype(BF)


def kernel(
    W, XY, NS, NT,
    obj, probe, amp_hbm, cur, prev, fr, fi,
    out_obj, out_probe,
    band_a, band_b, modes, amps, right_f, right_b, left_f, left_b,
    wave, stack, far, near, inten, win, numer, grads, weight, power, illum,
    pass_out, pass_in, total, fwd_out, fwd_in, rs_out, rs_in,
    core_out, core_in, plane_sum, plane_in, z_out, z_in, step_full,
    amp_sem, ag_s, ag_r, fw_s, fw_r, ps_s, ps_r,
    pz_s, pz_r, px_s, px_r, pc_s, pc_r,
    np_s, np_r, nf_s, nf_r, nr_s, nr_r,
    g1_s, g1_r, g2_s, g2_r, g3_s, g3_r, g4_s, g4_r, g5_s, g5_r,
):
    R = W // XY
    s = lax.axis_index("scan")
    t = lax.axis_index("tile")
    core = lax.rem(s, 2)
    zlo = lax.rem(s // 2, 2)
    q = s // 4
    right, left, opp = (lax.rem(t + d, NT) for d in (1, 3, 2))
    other_core = s + 1 - 2 * core
    other_zlo = s + 2 - 4 * zlo
    shard = pl.ds(pl.multiple_of(q * R, R), R)
    has_next = s < NS - 1
    has_prev = s > 0

    def copy_to(src, dst, ssem, rsem, scan, tile):
        return pltpu.make_async_remote_copy(
            src_ref=src, dst_ref=dst, send_sem=ssem, recv_sem=rsem,
            device_id=(scan, tile), device_id_type=MESH,
        )

    def column(step):
        to = lax.rem(q + step, XY)
        return to, to * 4 + zlo * 2 + core

    amp_copies = [
        pltpu.make_async_copy(amp_hbm.at[t + 4 * u], amps.at[u], amp_sem.at[u]) for u in range(2)
    ]
    for item in amp_copies:
        item.start()

    barrier = pltpu.get_barrier_semaphore()

    def greet(scan, tile):
        pl.semaphore_signal(barrier, inc=1, device_id=(scan, tile), device_id_type=MESH)

    for d in range(1, NT):
        greet(s, lax.rem(t + d, NT))
    for d in range(NT):
        greet(other_zlo, lax.rem(t + d, NT))
    greet(other_core, t)

    @pl.loop(1, XY)
    def _(step):
        greet(column(step)[1], t)

    @pl.when(has_next)
    def _():
        greet(s + 1, t)

    @pl.when(has_prev)
    def _():
        greet(s - 1, t)

    band_a[t] = obj[...].astype(BF)
    modes[0] = probe[...].astype(BF)
    pl.semaphore_wait(
        barrier, 2 * NT + XY - 1 + has_next.astype(jnp.int32) + has_prev.astype(jnp.int32)
    )

    to_right = [copy_to(band_a.at[t, p], band_a.at[t, p], ag_s.at[p], ag_r.at[p], s, right) for p in (0, 1)]
    to_left = [copy_to(band_a.at[t, p], band_a.at[t, p], ag_s.at[2 + p], ag_r.at[2 + p], s, left) for p in (0, 1)]
    from_left = [copy_to(band_a.at[left, p], band_a.at[left, p], ag_s.at[p], ag_r.at[p], s, right) for p in (0, 1)]
    from_right = [copy_to(band_a.at[right, p], band_a.at[right, p], ag_s.at[2 + p], ag_r.at[2 + p], s, left) for p in (0, 1)]
    on_right = copy_to(band_a.at[left, 0], band_a.at[left, 0], fw_s.at[0], fw_r.at[0], s, right)
    on_left = copy_to(band_a.at[right, 1], band_a.at[right, 1], fw_s.at[1], fw_r.at[1], s, left)
    opp_first = copy_to(band_a.at[opp, 0], band_a.at[opp, 0], fw_s.at[0], fw_r.at[0], s, right)
    opp_second = copy_to(band_a.at[opp, 1], band_a.at[opp, 1], fw_s.at[1], fw_r.at[1], s, left)

    def passed(block, slot):
        return copy_to(band_a.at[block], band_b.at[block], ps_s.at[slot], ps_r.at[slot], s - 1, t)

    def start_pass(block, slot):
        @pl.when(has_prev)
        def _():
            passed(block, slot).start()

    to_right[0].start()
    to_left[1].start()
    to_right[1].start()
    to_left[0].start()
    start_pass(t, 0)

    for d in range(1, NT):
        copy_to(
            modes.at[0, core, :, shard], modes.at[NT - d, core, :, shard],
            pz_s.at[d], pz_r.at[NT - d], s, lax.rem(t + d, NT),
        ).start()
    for d in range(1, NT):
        copy_to(
            modes.at[0, core, :, shard], modes.at[d, core, :, shard], pz_s.at[d], pz_r.at[d], s, t
        ).wait_recv()

    def over_columns(step):
        to, device = column(step)
        src = modes.at[pl.ds(1, NT - 1), core, :, shard]
        return copy_to(src, src, px_s.at[to], px_r.at[q], device, t)

    @pl.loop(1, XY)
    def _(step):
        over_columns(step).start()

    from_left[0].wait_recv()
    on_right.start()
    from_right[1].wait_recv()
    on_left.start()
    from_left[1].wait_recv()
    start_pass(left, 1)
    from_right[0].wait_recv()
    start_pass(right, 2)

    for table, ref in ((1.0, right_f), (-1.0, right_b)):
        sign = jnp.asarray(table, BF)
        ref[0:W, 0:W] = fr[...]
        ref[0:W, W:] = fi[...] * sign
        ref[W:, 0:W] = fi[...] * -sign
        ref[W:, W:] = fr[...]
    left_f[:, 0:W] = fr[...]
    left_f[:, W:] = -fi[...]
    left_b[:, 0:W] = fr[...]
    left_b[:, W:] = fi[...]

    opp_first.wait_recv()
    opp_second.wait_recv()
    start_pass(opp, 3)

    @pl.loop(1, XY)
    def _(step):
        source = lax.rem(q + step, XY)
        rows = pl.ds(pl.multiple_of(source * R, R), R)
        dst = modes.at[pl.ds(1, NT - 1), core, :, rows]
        copy_to(dst, dst, px_s.at[source], px_r.at[source], s, right).wait_recv()

    to_core = copy_to(
        modes.at[pl.ds(1, NT - 1), core], modes.at[pl.ds(1, NT - 1), core], pc_s, pc_r, other_core, t
    )
    from_core = copy_to(
        modes.at[pl.ds(1, NT - 1), 1 - core], modes.at[pl.ds(1, NT - 1), 1 - core], pc_s, pc_r, other_core, t
    )
    to_core.start()

    @pl.when(has_next)
    def _():
        for slot, block in enumerate((t, left, right, opp)):
            copy_to(band_a.at[block], band_b.at[block], ps_s.at[slot], ps_r.at[slot], s + 1, t).wait_recv()

    from_core.wait_recv()
    for item in amp_copies:
        item.wait()

    row_id = lax.broadcasted_iota(jnp.int32, (W, W), 0)
    col_id = lax.broadcasted_iota(jnp.int32, (W, W), 1)

    def place(table, slot, first):
        row = table[2 * slot] - first
        col = table[2 * slot + 1]
        live = jnp.where(slot < table[16], 1.0, 0.0).astype(F32)
        return row, lax.rem(col, W), col // W, live

    C = min(32, W)

    def by_rows(body):
        @pl.loop(0, W // C)
        def _(step):
            body(pl.ds(pl.multiple_of(step * C, C), C))

    def transform(right_table, left_table):
        half = jnp.dot(wave[...], right_table[...], preferred_element_type=F32).astype(BF)
        stack[0:W, :] = half
        stack[W:, 0:W] = half[:, W:]
        stack[W:, W:] = -half[:, 0:W]
        return jnp.dot(left_table[...], stack[...], preferred_element_type=F32)

    for u in range(2):
        row, lane, block, live = place(cur, t + 4 * u, s * W)
        after = jnp.minimum(block + 1, NT - 1)
        for p in range(2):
            upper = jnp.where(col_id >= lane, band_a[block, p].astype(F32), band_a[after, p].astype(F32))
            lower = jnp.where(col_id >= lane, band_b[block, p].astype(F32), band_b[after, p].astype(F32))
            merged = jnp.where(row_id >= row, upper, lower)
            merged = pltpu.roll(merged, lax.rem(W - row, W), 0)
            win[p] = pltpu.roll(merged, lax.rem(W - lane, W), 1)

        def start_slot(rows):
            square = live * (win[0, rows] * win[0, rows] + win[1, rows] * win[1, rows])
            weight[rows] = square if u == 0 else weight[rows] + square
            inten[rows] = jnp.zeros((C, W), F32)
            for p in range(2):
                numer[u, p, rows] = jnp.zeros((C, W), F32)

        by_rows(start_slot)

        @pl.loop(0, 2 * NT)
        def _(m):
            i, cc = m // 2, lax.rem(m, 2)

            def exit_rows(rows):
                pr = modes[i, cc, 0, rows].astype(F32)
                pi = modes[i, cc, 1, rows].astype(F32)
                wr, wi = win[0, rows], win[1, rows]
                wave[rows, 0:W] = (pr * wr - pi * wi).astype(BF)
                wave[rows, W:] = (pr * wi + pi * wr).astype(BF)
                if u == 0:
                    square = pr * pr + pi * pi
                    power[rows] = jnp.where(m == 0, 0.0, power[rows]) + square

            by_rows(exit_rows)
            far[m] = transform(right_f, left_f)

            def add_rows(rows):
                fa, fb = far[m, rows, 0:W], far[m, rows, W:]
                inten[rows] += fa * fa + fb * fb

            by_rows(add_rows)

        def factor_rows(rows):
            size = jnp.maximum(jnp.sqrt(inten[rows]), amp_floor)
            inten[rows] = live * (amps[u, rows].astype(F32) / size - 1.0)

        by_rows(factor_rows)

        @pl.loop(0, 2 * NT)
        def _(m):
            i, cc = m // 2, lax.rem(m, 2)

            def change_rows(rows):
                factor = inten[rows]
                wave[rows, 0:W] = (factor * far[m, rows, 0:W]).astype(BF)
                wave[rows, W:] = (factor * far[m, rows, W:]).astype(BF)

            by_rows(change_rows)
            near[...] = transform(right_b, left_b)

            def near_rows(rows):
                pr = modes[i, cc, 0, rows].astype(F32)
                pi = modes[i, cc, 1, rows].astype(F32)
                wr, wi = win[0, rows], win[1, rows]
                nr, ni = near[rows, 0:W], near[rows, W:]
                numer[u, 0, rows] += pr * nr + pi * ni
                numer[u, 1, rows] += pr * ni - pi * nr
                gr = wr * nr + wi * ni
                gi = wr * ni - wi * nr
                grads[i, cc, 0, rows] = gr if u == 0 else grads[i, cc, 0, rows] + gr
                grads[i, cc, 1, rows] = gi if u == 0 else grads[i, cc, 1, rows] + gi

            by_rows(near_rows)

        for p in range(2):
            rolled = pltpu.roll(numer[u, p], lane, 1)
            numer[u, p] = pltpu.roll(rolled, row, 0)

    def core_rows(rows):
        for i in range(NT):
            for p in range(2):
                core_out[2 * i + p, rows] = grads[i, 1 - core, p, rows].astype(BF)
        core_out[2 * NT, rows] = weight[rows].astype(BF)

    by_rows(core_rows)
    g1 = copy_to(core_out, core_in, g1_s, g1_r, other_core, t)
    g1.start()

    spots = [place(cur, t + 4 * u, s * W) for u in range(2)]

    def band_part(block, p, upper):
        value = 0.0
        for u, (row, lane, first, _) in enumerate(spots):
            cols = jnp.where(col_id >= lane, first, first + 1) == block
            rows = (row_id >= row) if upper else (row_id < row)
            value = value + jnp.where(cols & rows, numer[u, p], 0.0)
        return value

    def pass_sum(slot):
        return copy_to(pass_out.at[slot], pass_in.at[slot], np_s.at[slot], np_r.at[slot], s + 1, t)

    order = (opp, right, left, t)
    for slot, block in enumerate(order):
        for p in range(2):
            pass_out[slot, p] = band_part(block, p, False).astype(BF)

        @pl.when(has_next)
        def _():
            pass_sum(slot).start()

    g1.wait_recv()

    def sum_rows(rows):
        for i in range(NT):
            for p in range(2):
                k = 2 * i + p
                plane_sum[k, rows] = (grads[i, core, p, rows] + core_in[k, rows].astype(F32)).astype(BF)
        plane_sum[2 * NT, rows] = (weight[rows] + core_in[2 * NT, rows].astype(F32)).astype(BF)

    by_rows(sum_rows)

    def g2(step):
        to, device = column(step)
        rows = pl.ds(pl.multiple_of(to * R, R), R)
        return copy_to(plane_sum.at[:, rows], plane_in.at[q], g2_s.at[to], g2_r.at[q], device, t)

    @pl.loop(1, XY)
    def _(step):
        g2(step).start()

    for slot, block in enumerate(order):
        for p in range(2):
            total[slot, p] = band_part(block, p, True)

    illum[...] = jnp.zeros((W, W), F32)
    for table, first, upper in ((cur, s * W, True), (prev, (s - 1) * W, False)):
        @pl.loop(0, 8)
        def _(slot):
            row, lane, block, live = place(table, slot, first)
            row = lax.rem(row + W, W)
            moved = pltpu.roll(pltpu.roll(power[...], lane, 1), row, 0)
            cols = jnp.where(col_id >= lane, block, block + 1) == t
            rows = (row_id >= row) if upper else (row_id < row)
            illum[...] += live * jnp.where(cols & rows, moved, 0.0)

    def take_pass(slot):
        @pl.when(has_prev)
        def _():
            copy_to(pass_out.at[slot], pass_in.at[slot], np_s.at[slot], np_r.at[slot], s - 1, t).wait_recv()
            for p in range(2):
                total[slot, p] += pass_in[slot, p].astype(F32)

    take_pass(0)
    forwards = []
    for p, to in ((0, right), (1, left)):
        fwd_out[p] = total[0, p].astype(BF)
        item = copy_to(fwd_out.at[p], fwd_in.at[p], nf_s.at[p], nf_r.at[p], s, to)
        item.start()
        forwards.append(item)
    sends = {}
    for way, to in ((0, right), (1, left)):
        for p in range(2):
            sends[way, p] = copy_to(
                rs_out.at[way, p], rs_in.at[way, p], nr_s.at[way, p], nr_r.at[way, p], s, to
            )
    take_pass(1)
    rs_out[0, 1] = total[1, 1].astype(BF)
    sends[0, 1].start()
    take_pass(2)
    rs_out[1, 0] = total[2, 0].astype(BF)
    sends[1, 0].start()
    forwards[0].wait_recv()
    rs_out[0, 0] = (total[1, 0] + fwd_in[0].astype(F32)).astype(BF)
    sends[0, 0].start()
    forwards[1].wait_recv()
    rs_out[1, 1] = (total[2, 1] + fwd_in[1].astype(F32)).astype(BF)
    sends[1, 1].start()

    @pl.loop(1, XY)
    def _(step):
        source = lax.rem(q + step, XY)
        copy_to(plane_sum.at[:, shard], plane_in.at[source], g2_s.at[source], g2_r.at[source], s, right).wait_recv()

    plane_in[q] = plane_sum[:, shard]
    for k in range(2 * NT + 1):
        value = plane_in[0, k].astype(F32)
        for source in range(1, XY):
            value = value + plane_in[source, k].astype(F32)
        if k < 2 * NT:
            z_out[k // 2, k % 2] = value
        else:
            for i in range(NT):
                z_out[i, 2] = value
    me_z = 2 * t + zlo
    z_in[me_z] = z_out[0]
    z_copies = []
    for flip in range(2):
        for d in range(NT):
            if flip == 0 and d == 0:
                continue
            k = flip * NT + d
            scan = other_zlo if flip else s
            item = copy_to(z_out.at[d], z_in.at[me_z], g3_s.at[k], g3_r.at[me_z], scan, lax.rem(t + d, NT))
            item.start()
            z_copies.append(item)

    take_pass(3)
    for item in sends.values():
        item.wait_recv()
    for p in range(2):
        value = total[3, p] + (rs_in[0, p].astype(F32) + rs_in[1, p].astype(F32))
        out_obj[p] = obj[p] + value / (illum[...] + damping)

    for flip in range(2):
        for d in range(NT):
            if flip == 0 and d == 0:
                continue
            source = 2 * lax.rem(t + d, NT) + (1 - zlo if flip else zlo)
            copy_to(z_out.at[d], z_in.at[source], g3_s.at[d], g3_r.at[source], s, right).wait_recv()
    summed = [z_in[0, k] for k in range(3)]
    for source in range(1, 2 * NT):
        summed = [summed[k] + z_in[source, k] for k in range(3)]
    for p in range(2):
        step_full[core, p, shard] = summed[p] / (summed[2] + damping)

    def g4(step):
        to, device = column(step)
        src = step_full.at[core, :, shard]
        return copy_to(src, src, g4_s.at[to], g4_r.at[q], device, t)

    @pl.loop(1, XY)
    def _(step):
        g4(step).start()

    @pl.loop(1, XY)
    def _(step):
        source = lax.rem(q + step, XY)
        rows = pl.ds(pl.multiple_of(source * R, R), R)
        dst = step_full.at[core, :, rows]
        copy_to(dst, dst, g4_s.at[source], g4_r.at[source], s, right).wait_recv()

    g5 = copy_to(step_full.at[core], step_full.at[core], g5_s, g5_r, other_core, t)
    g5.start()
    copy_to(step_full.at[1 - core], step_full.at[1 - core], g5_s, g5_r, other_core, t).wait_recv()
    out_probe[...] = step_full[...]

    for item in to_right + to_left + [on_right, on_left, to_core, g1, g5] + forwards + z_copies + list(sends.values()):
        item.wait_send()
    for d in range(1, NT):
        copy_to(
            modes.at[0, core, :, shard], modes.at[NT - d, core, :, shard],
            pz_s.at[d], pz_r.at[NT - d], s, lax.rem(t + d, NT),
        ).wait_send()

    @pl.loop(1, XY)
    def _(step):
        over_columns(step).wait_send()
        g2(step).wait_send()
        g4(step).wait_send()

    @pl.when(has_prev)
    def _():
        for slot, block in enumerate((t, left, right, opp)):
            passed(block, slot).wait_send()

    @pl.when(has_next)
    def _():
        for slot in range(NT):
            pass_sum(slot).wait_send()


def shards(NS, NT, object_field, probe_modes, amplitudes, positions, counts):
    W = amplitudes.shape[1]
    XY = NS // 4
    R = W // XY
    fr, fi = dft_tables(W)
    table = jnp.concatenate([positions.reshape(-1), counts])
    before = lax.ppermute(table, "scan", [(k, k + 1) for k in range(NS - 1)])
    vmem = pl.BlockSpec(memory_space=pltpu.VMEM)
    smem = pl.BlockSpec(memory_space=pltpu.SMEM)
    dma = pltpu.SemaphoreType.DMA

    def buf(*shape, dtype=F32):
        return pltpu.VMEM(shape, dtype)

    scratch = [
        buf(NT, 2, W, W, dtype=BF), buf(NT, 2, W, W, dtype=BF), buf(NT, 2, 2, W, W, dtype=BF),
        buf(2, W, W, dtype=BF), buf(2 * W, 2 * W, dtype=BF), buf(2 * W, 2 * W, dtype=BF),
        buf(W, 2 * W, dtype=BF), buf(W, 2 * W, dtype=BF),
        buf(W, 2 * W, dtype=BF), buf(2 * W, 2 * W, dtype=BF), buf(2 * NT, W, 2 * W), buf(W, 2 * W),
        buf(W, W), buf(2, W, W), buf(2, 2, W, W), buf(NT, 2, 2, W, W), buf(W, W), buf(W, W), buf(W, W),
        buf(NT, 2, W, W, dtype=BF), buf(NT, 2, W, W, dtype=BF), buf(NT, 2, W, W),
        buf(2, W, W, dtype=BF), buf(2, W, W, dtype=BF), buf(2, 2, W, W, dtype=BF), buf(2, 2, W, W, dtype=BF),
        buf(2 * NT + 1, W, W, dtype=BF), buf(2 * NT + 1, W, W, dtype=BF), buf(2 * NT + 1, W, W, dtype=BF),
        buf(XY, 2 * NT + 1, R, W, dtype=BF), buf(NT, 3, R, W), buf(2 * NT, 3, R, W), buf(2, 2, W, W),
        dma((2,)), dma((4,)), dma((4,)), dma((2,)), dma((2,)), dma((4,)), dma((4,)),
        dma((NT,)), dma((NT,)), dma((XY,)), dma((XY,)), dma, dma,
        dma((NT,)), dma((NT,)), dma((2,)), dma((2,)), dma((2, 2)), dma((2, 2)),
        dma, dma, dma((XY,)), dma((XY,)), dma((2 * NT,)), dma((2 * NT,)), dma((XY,)), dma((XY,)), dma, dma,
    ]
    new_object, probe_step = pl.pallas_call(
        functools.partial(kernel, W, XY, NS, NT),
        out_shape=(
            jax.ShapeDtypeStruct(object_field.shape, F32),
            jax.ShapeDtypeStruct(probe_modes.shape, F32),
        ),
        in_specs=[vmem, vmem, pl.BlockSpec(memory_space=pl.ANY), smem, smem, vmem, vmem],
        out_specs=(vmem, vmem),
        scratch_shapes=scratch,
        compiler_params=pltpu.CompilerParams(
            collective_id=0, has_side_effects=True, vmem_limit_bytes=58 * 1024 * 1024
        ),
    )(object_field, probe_modes, amplitudes, table, before, jnp.asarray(fr), jnp.asarray(fi))
    return new_object, probe_step


def solution(mesh):
    placed = (
        P(None, "scan", "tile"),
        P("tile", None, None, None),
        P("scan", None, None),
        P("scan", None),
        P("scan"),
    )
    return jax.shard_map(
        functools.partial(shards, mesh.shape["scan"], mesh.shape["tile"]),
        mesh=mesh,
        in_specs=placed,
        out_specs=(P(None, "scan", "tile"), P("tile", None, None, None)),
        check_vma=False,
    )
```

```python
import functools
import math

import jax
import jax.numpy as jnp
import numpy as np
from jax import lax
from jax.experimental import pallas as pl
from jax.experimental.pallas import tpu as pltpu
from jax.sharding import PartitionSpec as P

damping = 1.0
amp_floor = 0.5
MESH = pl.DeviceIdType.MESH
BF = jnp.bfloat16
F32 = jnp.float32


def dft_tables(width):
    index = np.arange(width)
    angle = (index[:, None] * index[None, :] % width) * (2.0 * math.pi / width)
    scale = 1.0 / math.sqrt(width)
    return (np.cos(angle) * scale).astype(BF), (-np.sin(angle) * scale).astype(BF)


def kernel(
    W, XY, NS, NT,
    obj_hbm, probe_hbm, amp_hbm, pos, cnt, pos_hbm, cnt_hbm, fr, fi,
    out_obj, out_probe,
    obj, probe, band_a, band_b, modes, amps, right_f, right_b, left_f, left_b,
    wave, stack, far, near, inten, win, numer, grads, weight, power, illum,
    pos_land, cnt_land, prev_pos, prev_cnt,
    pass_out, pass_in, total, fwd_out, fwd_in, rs_out, rs_in,
    core_out, core_in, plane_sum, plane_in, z_out, z_in, step_full,
    in_sem, sm_sem, tb_s, tb_r, ag_s, ag_r, fw_s, fw_r, ps_s, ps_r,
    pz_s, pz_r, px_s, px_r, pc_s, pc_r,
    np_s, np_r, nf_s, nf_r, nr_s, nr_r,
    g1_s, g1_r, g2_s, g2_r, gw_s, gw_r, g3_s, g3_r, g4_s, g4_r, g5_s, g5_r,
):
    R = W // XY
    C = min(32, W)
    s = lax.axis_index("scan")
    t = lax.axis_index("tile")
    core = lax.rem(s, 2)
    zlo = lax.rem(s // 2, 2)
    q = s // 4
    right, left, opp = (lax.rem(t + d, NT) for d in (1, 3, 2))
    other_core = s + 1 - 2 * core
    other_zlo = s + 2 - 4 * zlo
    shard = pl.ds(pl.multiple_of(q * R, R), R)
    has_next = s < NS - 1
    has_prev = s > 0

    def copy_to(src, dst, ssem, rsem, scan, tile):
        return pltpu.make_async_remote_copy(
            src_ref=src, dst_ref=dst, send_sem=ssem, recv_sem=rsem,
            device_id=(scan, tile), device_id_type=MESH,
        )

    def column(step):
        to = lax.rem(q + step, XY)
        return to, to * 4 + zlo * 2 + core

    def by_rows(body):
        @pl.loop(0, W // C)
        def _(step):
            body(pl.ds(pl.multiple_of(step * C, C), C))

    local = [
        pltpu.make_async_copy(src, dst, in_sem.at[k])
        for k, (src, dst) in enumerate((
            (obj_hbm, obj), (probe_hbm, probe), (amp_hbm.at[t], amps.at[0]), (amp_hbm.at[t + 4], amps.at[1]),
        ))
    ]
    for item in local:
        item.start()

    barrier = pltpu.get_barrier_semaphore()

    def greet(scan, tile):
        pl.semaphore_signal(barrier, inc=1, device_id=(scan, tile), device_id_type=MESH)

    for d in range(1, NT):
        greet(s, lax.rem(t + d, NT))
    for d in range(NT):
        greet(other_zlo, lax.rem(t + d, NT))
    greet(other_core, t)

    @pl.loop(1, XY)
    def _(step):
        greet(column(step)[1], t)

    up_tile = lax.rem(t + jnp.where((core == 0) & (zlo == 1), 1, 0) + jnp.where((core == 0) & (zlo == 0), NT - 1, 0), NT)
    up_tile = jnp.where((core == 0), up_tile, t)
    down_tile = lax.rem(t + jnp.where((core == 1) & (zlo == 0), NT - 1, 0) + jnp.where((core == 1) & (zlo == 1), 1, 0), NT)

    @pl.when(has_next)
    def _():
        greet(s + 1, t)
        greet(s + 1, down_tile)

    @pl.when(has_prev)
    def _():
        greet(s - 1, t)
        greet(s - 1, up_tile)

    local[1].wait()
    modes[0] = probe[...].astype(BF)
    local[0].wait()
    band_a[t] = obj[...].astype(BF)
    pl.semaphore_wait(
        barrier, 2 * NT + XY - 1 + 2 * has_next.astype(jnp.int32) + 2 * has_prev.astype(jnp.int32)
    )

    for d in range(1, NT):
        copy_to(
            modes.at[0, core, :, shard], modes.at[NT - d, core, :, shard],
            pz_s.at[d], pz_r.at[NT - d], s, lax.rem(t + d, NT),
        ).start()

    to_right = [copy_to(band_a.at[t, p], band_a.at[t, p], ag_s.at[p], ag_r.at[p], s, right) for p in (0, 1)]
    to_left = [copy_to(band_a.at[t, p], band_a.at[t, p], ag_s.at[2 + p], ag_r.at[2 + p], s, left) for p in (0, 1)]
    from_left = [copy_to(band_a.at[left, p], band_a.at[left, p], ag_s.at[p], ag_r.at[p], s, right) for p in (0, 1)]
    from_right = [copy_to(band_a.at[right, p], band_a.at[right, p], ag_s.at[2 + p], ag_r.at[2 + p], s, left) for p in (0, 1)]
    on_right = copy_to(band_a.at[left, 0], band_a.at[left, 0], fw_s.at[0], fw_r.at[0], s, right)
    on_left = copy_to(band_a.at[right, 1], band_a.at[right, 1], fw_s.at[1], fw_r.at[1], s, left)
    opp_first = copy_to(band_a.at[opp, 0], band_a.at[opp, 0], fw_s.at[0], fw_r.at[0], s, right)
    opp_second = copy_to(band_a.at[opp, 1], band_a.at[opp, 1], fw_s.at[1], fw_r.at[1], s, left)

    def passed(block, p):
        return copy_to(
            band_a.at[block, p], band_b.at[block, p], ps_s.at[block, p], ps_r.at[block, p],
            s - 1, up_tile if p == 0 else t,
        )

    def start_pass(block, *planes):
        @pl.when(has_prev)
        def _():
            for p in planes:
                passed(block, p).start()

    to_right[0].start()
    to_left[1].start()
    to_right[1].start()
    to_left[0].start()
    start_pass(t, 0, 1)

    tables = [
        copy_to(src, dst, tb_s.at[k], tb_r.at[k], s + 1, t)
        for k, (src, dst) in enumerate(((pos_hbm, pos_land), (cnt_hbm, cnt_land)))
    ]

    @pl.when(has_next)
    def _():
        for item in tables:
            item.start()

    for d in range(1, NT):
        copy_to(
            modes.at[0, core, :, shard], modes.at[d, core, :, shard], pz_s.at[d], pz_r.at[d], s, t
        ).wait_recv()

    def over_columns(step):
        to, device = column(step)
        src = modes.at[pl.ds(1, NT - 1), core, :, shard]
        return copy_to(src, src, px_s.at[to], px_r.at[q], device, t)

    @pl.loop(1, XY)
    def _(step):
        over_columns(step).start()

    from_left[0].wait_recv()
    on_right.start()
    from_right[1].wait_recv()
    on_left.start()
    start_pass(left, 0)
    start_pass(right, 1)
    from_left[1].wait_recv()
    start_pass(left, 1)
    from_right[0].wait_recv()
    start_pass(right, 0)

    for table, ref in ((1.0, right_f), (-1.0, right_b)):
        sign = jnp.asarray(table, BF)
        ref[0:W, 0:W] = fr[...]
        ref[0:W, W:] = fi[...] * sign
        ref[W:, 0:W] = fi[...] * -sign
        ref[W:, W:] = fr[...]
    left_f[:, 0:W] = fr[...]
    left_f[:, W:] = -fi[...]
    left_b[:, 0:W] = fr[...]
    left_b[:, W:] = fi[...]

    opp_first.wait_recv()
    start_pass(opp, 0)
    opp_second.wait_recv()
    start_pass(opp, 1)

    @pl.loop(1, XY)
    def _(step):
        source = lax.rem(q + step, XY)
        rows = pl.ds(pl.multiple_of(source * R, R), R)
        dst = modes.at[pl.ds(1, NT - 1), core, :, rows]
        copy_to(dst, dst, px_s.at[source], px_r.at[source], s, right).wait_recv()

    def to_core(i):
        return copy_to(modes.at[i, core], modes.at[i, core], pc_s.at[i], pc_r.at[i], other_core, t)

    for i in range(1, NT):
        to_core(i).start()

    prev_copies = [
        pltpu.make_async_copy(src, dst, sm_sem.at[k])
        for k, (src, dst) in enumerate(((pos_land, prev_pos), (cnt_land, prev_cnt)))
    ]

    @pl.when(has_prev)
    def _():
        for item, copy in zip(tables, prev_copies):
            item.wait_recv()
            copy.start()

    for item in local[2:]:
        item.wait()

    @pl.when(has_next)
    def _():
        for block in (t, left, right, opp):
            for p in range(2):
                copy_to(
                    band_a.at[block, p], band_b.at[block, p], ps_s.at[block, p], ps_r.at[block, p], s + 1, t
                ).wait_recv()

    row_id = lax.broadcasted_iota(jnp.int32, (W, W), 0)
    col_id = lax.broadcasted_iota(jnp.int32, (W, W), 1)

    def place(slot):
        row, col = pos[slot, 0] - s * W, pos[slot, 1]
        live = jnp.where(slot < cnt[0], 1.0, 0.0).astype(F32)
        return row, lax.rem(col, W), col // W, live

    def place_prev(slot):
        row = jnp.where(has_prev, prev_pos[slot, 0] - (s - 1) * W, 0)
        col = jnp.where(has_prev, prev_pos[slot, 1], 0)
        live = jnp.where(has_prev & (slot < prev_cnt[0]), 1.0, 0.0).astype(F32)
        return row, lax.rem(col, W), col // W, live

    def transform(right_table, left_table):
        half = jnp.dot(wave[...], right_table[...], preferred_element_type=F32).astype(BF)
        stack[0:W, :] = half
        stack[W:, 0:W] = half[:, W:]
        stack[W:, W:] = -half[:, 0:W]
        return jnp.dot(left_table[...], stack[...], preferred_element_type=F32)

    def pass_sum(u):
        return copy_to(pass_out.at[u], pass_in.at[u], np_s.at[u], np_r.at[u], s + 1, t)

    last = 2 * NT

    def g1(i):
        planes = pl.ds(2 * i, 2)
        return copy_to(core_out.at[planes], core_in.at[planes], g1_s.at[i], g1_r.at[i], other_core, t)

    g1w = copy_to(core_out.at[last], core_in.at[last], g1_s.at[NT], g1_r.at[NT], other_core, t)

    def shard_of(to):
        return pl.ds(pl.multiple_of(to * R, R), R)

    def g2(i, step):
        to, device = column(step)
        planes = pl.ds(2 * i, 2)
        return copy_to(
            plane_sum.at[planes, shard_of(to)], plane_in.at[q, planes], g2_s.at[i, to], g2_r.at[i, q], device, t
        )

    def g2w(step):
        to, device = column(step)
        return copy_to(plane_sum.at[last, shard_of(to)], plane_in.at[q, last], gw_s.at[to], gw_r.at[q], device, t)

    for u in range(2):
        row, lane, block, live = place(t + 4 * u)
        after = jnp.minimum(block + 1, NT - 1)
        for p in range(2):
            upper = jnp.where(col_id >= lane, band_a[block, p].astype(F32), band_a[after, p].astype(F32))
            lower = jnp.where(col_id >= lane, band_b[block, p].astype(F32), band_b[after, p].astype(F32))
            merged = jnp.where(row_id >= row, upper, lower)
            merged = pltpu.roll(merged, lax.rem(W - row, W), 0)
            win[p] = pltpu.roll(merged, lax.rem(W - lane, W), 1)

        def start_slot(rows):
            square = live * (win[0, rows] * win[0, rows] + win[1, rows] * win[1, rows])
            if u == 0:
                weight[rows] = square
            else:
                weight[rows] += square
                core_out[last, rows] = weight[rows].astype(BF)
            inten[rows] = jnp.zeros((C, W), F32)
            for p in range(2):
                numer[u, p, rows] = jnp.zeros((C, W), F32)

        by_rows(start_slot)
        if u == 1:
            g1w.start()

        @pl.loop(0, 2 * NT)
        def _(m):
            i, cc = m // 2, lax.rem(m, 2)
            if u == 0:
                @pl.when((i > 0) & (cc == 0))
                def _():
                    copy_to(modes.at[i, 1 - core], modes.at[i, 1 - core], pc_s.at[i], pc_r.at[i], other_core, t).wait_recv()

            def exit_rows(rows):
                pr = modes[i, cc, 0, rows].astype(F32)
                pi = modes[i, cc, 1, rows].astype(F32)
                wr, wi = win[0, rows], win[1, rows]
                wave[rows, 0:W] = (pr * wr - pi * wi).astype(BF)
                wave[rows, W:] = (pr * wi + pi * wr).astype(BF)
                if u == 0:
                    square = pr * pr + pi * pi
                    power[rows] = jnp.where(m == 0, 0.0, power[rows]) + square

            by_rows(exit_rows)
            far[m] = transform(right_f, left_f)

            def add_rows(rows):
                fa, fb = far[m, rows, 0:W], far[m, rows, W:]
                inten[rows] += fa * fa + fb * fb

            by_rows(add_rows)

        def factor_rows(rows):
            size = jnp.maximum(jnp.sqrt(inten[rows]), amp_floor)
            inten[rows] = live * (amps[u, rows].astype(F32) / size - 1.0)

        by_rows(factor_rows)

        if u == 1:
            g1w.wait_recv()

            def weight_rows(rows):
                plane_sum[last, rows] = (weight[rows] + core_in[last, rows].astype(F32)).astype(BF)

            by_rows(weight_rows)

            @pl.loop(1, XY)
            def _(step):
                g2w(step).start()

        @pl.loop(0, NT)
        def _(i):
            for turn in range(2):
                cc = core if turn else 1 - core
                m = 2 * i + cc

                def change_rows(rows):
                    factor = inten[rows]
                    wave[rows, 0:W] = (factor * far[m, rows, 0:W]).astype(BF)
                    wave[rows, W:] = (factor * far[m, rows, W:]).astype(BF)

                by_rows(change_rows)
                near[...] = transform(right_b, left_b)

                def near_rows(rows):
                    pr = modes[i, cc, 0, rows].astype(F32)
                    pi = modes[i, cc, 1, rows].astype(F32)
                    wr, wi = win[0, rows], win[1, rows]
                    nr, ni = near[rows, 0:W], near[rows, W:]
                    numer[u, 0, rows] += pr * nr + pi * ni
                    numer[u, 1, rows] += pr * ni - pi * nr
                    both = (wr * nr + wi * ni, wr * ni - wi * nr)
                    for p in range(2):
                        if u == 0:
                            grads[i, cc, p, rows] = both[p]
                        elif turn == 0:
                            core_out[2 * i + p, rows] = (grads[i, cc, p, rows] + both[p]).astype(BF)
                        else:
                            grads[i, cc, p, rows] += both[p]

                by_rows(near_rows)
                if u == 1 and turn == 0:
                    g1(i).start()

            if u == 1:
                g1(i).wait_recv()

                def sum_rows(rows):
                    for p in range(2):
                        k = 2 * i + p
                        plane_sum[k, rows] = (grads[i, core, p, rows] + core_in[k, rows].astype(F32)).astype(BF)

                by_rows(sum_rows)

                @pl.loop(1, XY)
                def _(step):
                    g2(i, step).start()

        for p in range(2):
            rolled = pltpu.roll(numer[u, p], lane, 1)
            rolled = pltpu.roll(rolled, row, 0)
            numer[u, p] = rolled
            pass_out[u, p] = rolled.astype(BF)

        @pl.when(has_next)
        def _():
            pass_sum(u).start()

    @pl.when(has_prev)
    def _():
        for item in prev_copies:
            item.wait()

    illum[...] = jnp.zeros((W, W), F32)
    for where_is, upper in ((place, True), (place_prev, False)):
        @pl.loop(0, 8)
        def _(slot):
            row, lane, block, live = where_is(slot)
            moved = pltpu.roll(pltpu.roll(power[...], lane, 1), row, 0)
            cols = jnp.where(col_id >= lane, block, block + 1) == t
            rows = (row_id >= row) if upper else (row_id < row)
            illum[...] += live * jnp.where(cols & rows, moved, 0.0)

    @pl.loop(1, XY)
    def _(step):
        source = lax.rem(q + step, XY)
        copy_to(plane_sum.at[last, shard], plane_in.at[source, last], gw_s.at[source], gw_r.at[source], s, right).wait_recv()

        @pl.loop(0, NT)
        def _(i):
            planes = pl.ds(2 * i, 2)
            copy_to(
                plane_sum.at[planes, shard], plane_in.at[source, planes],
                g2_s.at[i, source], g2_r.at[i, source], s, right,
            ).wait_recv()

    plane_in[q] = plane_sum[:, shard]
    for k in range(2 * NT + 1):
        value = plane_in[0, k].astype(F32)
        for source in range(1, XY):
            value = value + plane_in[source, k].astype(F32)
        if k < 2 * NT:
            z_out[k // 2, k % 2] = value.astype(BF)
        else:
            for i in range(NT):
                z_out[i, 2] = value.astype(BF)
    me_z = 2 * t + zlo
    z_in[me_z] = z_out[0]
    z_copies = []
    for flip in range(2):
        for d in range(NT):
            if flip == 0 and d == 0:
                continue
            k = flip * NT + d
            scan = other_zlo if flip else s
            item = copy_to(z_out.at[d], z_in.at[me_z], g3_s.at[k], g3_r.at[me_z], scan, lax.rem(t + d, NT))
            item.start()
            z_copies.append(item)

    @pl.when(has_prev)
    def _():
        for u in range(2):
            copy_to(pass_out.at[u], pass_in.at[u], np_s.at[u], np_r.at[u], s - 1, t).wait_recv()

    order = (opp, right, left, t)
    spots = [place(t + 4 * u) for u in range(2)] + [place_prev(t + 4 * u) for u in range(2)]

    def total_rows(rows):
        start = rows.start
        row_at = lax.broadcasted_iota(jnp.int32, (C, W), 0) + start
        col_at = lax.broadcasted_iota(jnp.int32, (C, W), 1)
        owners = [jnp.where(col_at >= lane, first, first + 1) for _, lane, first, _ in spots]
        for p in range(2):
            values = [numer[u, p, rows] for u in range(2)] + [pass_in[u, p, rows].astype(F32) for u in range(2)]
            values = [
                jnp.where(row_at >= spot[0] if k < 2 else row_at < spot[0], value, 0.0)
                for k, (value, spot) in enumerate(zip(values, spots))
            ]
            for slot, block in enumerate(order):
                value = 0.0
                for k in range(4):
                    value = value + jnp.where(owners[k] == block, values[k], 0.0)
                if slot == 0:
                    fwd_out[p, rows] = value.astype(BF)
                elif slot == 3:
                    total[2, p, rows] = value
                elif p == 2 - slot:
                    rs_out[slot - 1, p, rows] = value.astype(BF)
                else:
                    total[slot - 1, 0, rows] = value

    by_rows(total_rows)
    forwards = []
    for p, to in ((0, right), (1, left)):
        item = copy_to(fwd_out.at[p], fwd_in.at[p], nf_s.at[p], nf_r.at[p], s, to)
        item.start()
        forwards.append(item)
    sends = {}
    for way, to in ((0, right), (1, left)):
        for p in range(2):
            sends[way, p] = copy_to(
                rs_out.at[way, p], rs_in.at[way, p], nr_s.at[way, p], nr_r.at[way, p], s, to
            )
    sends[0, 1].start()
    sends[1, 0].start()
    for way in range(2):
        forwards[way].wait_recv()
        rs_out[way, way] = (total[way, 0] + fwd_in[way].astype(F32)).astype(BF)
        sends[way, way].start()

    for flip in range(2):
        for d in range(NT):
            if flip == 0 and d == 0:
                continue
            source = 2 * lax.rem(t + d, NT) + (1 - zlo if flip else zlo)
            copy_to(z_out.at[d], z_in.at[source], g3_s.at[d], g3_r.at[source], s, right).wait_recv()
    summed = [z_in[0, k].astype(F32) for k in range(3)]
    for source in range(1, 2 * NT):
        summed = [summed[k] + z_in[source, k].astype(F32) for k in range(3)]
    for p in range(2):
        step_full[core, p, shard] = summed[p] / (summed[2] + damping)

    def g4(step):
        to, device = column(step)
        src = step_full.at[core, :, shard]
        return copy_to(src, src, g4_s.at[to], g4_r.at[q], device, t)

    @pl.loop(1, XY)
    def _(step):
        g4(step).start()

    @pl.loop(1, XY)
    def _(step):
        source = lax.rem(q + step, XY)
        dst = step_full.at[core, :, shard_of(source)]
        copy_to(dst, dst, g4_s.at[source], g4_r.at[source], s, right).wait_recv()

    g5 = copy_to(step_full.at[core], step_full.at[core], g5_s, g5_r, other_core, t)
    g5.start()

    for item in sends.values():
        item.wait_recv()

    def object_rows(rows):
        scale = illum[rows] + damping
        for p in range(2):
            value = total[2, p, rows] + (rs_in[0, p, rows].astype(F32) + rs_in[1, p, rows].astype(F32))
            out_obj[p, rows] = obj[p, rows] + value / scale

    by_rows(object_rows)
    copy_to(step_full.at[1 - core], step_full.at[1 - core], g5_s, g5_r, other_core, t).wait_recv()
    out_probe[...] = step_full[...]

    for item in to_right + to_left + [on_right, on_left, g1w, g5] + forwards + z_copies + list(sends.values()):
        item.wait_send()
    for d in range(1, NT):
        copy_to(
            modes.at[0, core, :, shard], modes.at[NT - d, core, :, shard],
            pz_s.at[d], pz_r.at[NT - d], s, lax.rem(t + d, NT),
        ).wait_send()
        to_core(d).wait_send()

    @pl.loop(0, NT)
    def _(i):
        g1(i).wait_send()

    @pl.loop(1, XY)
    def _(step):
        over_columns(step).wait_send()
        g2w(step).wait_send()
        g4(step).wait_send()

        @pl.loop(0, NT)
        def _(i):
            g2(i, step).wait_send()

    @pl.when(has_prev)
    def _():
        for block in (t, left, right, opp):
            for p in range(2):
                passed(block, p).wait_send()

    @pl.when(has_next)
    def _():
        for item in tables:
            item.wait_send()
        for u in range(2):
            pass_sum(u).wait_send()


def shards(NS, NT, object_field, probe_modes, amplitudes, positions, counts):
    W = amplitudes.shape[1]
    XY = NS // 4
    R = W // XY
    fr, fi = dft_tables(W)
    vmem = pl.BlockSpec(memory_space=pltpu.VMEM)
    smem = pl.BlockSpec(memory_space=pltpu.SMEM)
    hbm = pl.BlockSpec(memory_space=pl.ANY)
    dma = pltpu.SemaphoreType.DMA

    def buf(*shape, dtype=F32):
        return pltpu.VMEM(shape, dtype)

    scratch = [
        buf(2, W, W), buf(2, 2, W, W),
        buf(NT, 2, W, W, dtype=BF), buf(NT, 2, W, W, dtype=BF), buf(NT, 2, 2, W, W, dtype=BF),
        buf(2, W, W, dtype=BF), buf(2 * W, 2 * W, dtype=BF), buf(2 * W, 2 * W, dtype=BF),
        buf(W, 2 * W, dtype=BF), buf(W, 2 * W, dtype=BF),
        buf(W, 2 * W, dtype=BF), buf(2 * W, 2 * W, dtype=BF), buf(2 * NT, W, 2 * W), buf(W, 2 * W),
        buf(W, W), buf(2, W, W), buf(2, 2, W, W), buf(NT, 2, 2, W, W), buf(W, W), buf(W, W), buf(W, W),
        buf(8, 2, dtype=jnp.int32), buf(1, dtype=jnp.int32),
        pltpu.SMEM((8, 2), jnp.int32), pltpu.SMEM((1,), jnp.int32),
        buf(2, 2, W, W, dtype=BF), buf(2, 2, W, W, dtype=BF), buf(3, 2, W, W),
        buf(2, W, W, dtype=BF), buf(2, W, W, dtype=BF), buf(2, 2, W, W, dtype=BF), buf(2, 2, W, W, dtype=BF),
        buf(2 * NT + 1, W, W, dtype=BF), buf(2 * NT + 1, W, W, dtype=BF), buf(2 * NT + 1, W, W, dtype=BF),
        buf(XY, 2 * NT + 1, R, W, dtype=BF), buf(NT, 3, R, W, dtype=BF), buf(2 * NT, 3, R, W, dtype=BF),
        buf(2, 2, W, W),
        dma((4,)), dma((2,)), dma((2,)), dma((2,)), dma((4,)), dma((4,)), dma((2,)), dma((2,)), dma((4, 2)), dma((4, 2)),
        dma((NT,)), dma((NT,)), dma((XY,)), dma((XY,)), dma((NT,)), dma((NT,)),
        dma((2,)), dma((2,)), dma((2,)), dma((2,)), dma((2, 2)), dma((2, 2)),
        dma((NT + 1,)), dma((NT + 1,)), dma((NT, XY)), dma((NT, XY)), dma((XY,)), dma((XY,)),
        dma((2 * NT,)), dma((2 * NT,)), dma((XY,)), dma((XY,)), dma, dma,
    ]
    new_object, probe_step = pl.pallas_call(
        functools.partial(kernel, W, XY, NS, NT),
        out_shape=(
            jax.ShapeDtypeStruct(object_field.shape, F32),
            jax.ShapeDtypeStruct(probe_modes.shape, F32),
        ),
        in_specs=[hbm, hbm, hbm, smem, smem, vmem, vmem, vmem, vmem],
        out_specs=(vmem, vmem),
        scratch_shapes=scratch,
        compiler_params=pltpu.CompilerParams(
            collective_id=0, has_side_effects=True, vmem_limit_bytes=58 * 1024 * 1024
        ),
    )(object_field, probe_modes, amplitudes, positions, counts, positions, counts, jnp.asarray(fr), jnp.asarray(fi))
    return new_object, probe_step


def solution(mesh):
    placed = (
        P(None, "scan", "tile"),
        P("tile", None, None, None),
        P("scan", None, None),
        P("scan", None),
        P("scan"),
    )
    return jax.shard_map(
        functools.partial(shards, mesh.shape["scan"], mesh.shape["tile"]),
        mesh=mesh,
        in_specs=placed,
        out_specs=(P(None, "scan", "tile"), P("tile", None, None, None)),
        check_vma=False,
    )
```

```python
import functools
import math

import jax
import jax.numpy as jnp
import numpy as np
from jax import lax
from jax.experimental import pallas as pl
from jax.experimental.pallas import tpu as pltpu
from jax.sharding import PartitionSpec as P

damping = 1.0
amp_floor = 0.5
MESH = pl.DeviceIdType.MESH
BF = jnp.bfloat16
F32 = jnp.float32


def dft_tables(width):
    index = np.arange(width)
    angle = (index[:, None] * index[None, :] % width) * (2.0 * math.pi / width)
    scale = 1.0 / math.sqrt(width)
    return (np.cos(angle) * scale).astype(BF), (-np.sin(angle) * scale).astype(BF)


def kernel(
    W, XY, NS, NT,
    obj_hbm, probe_hbm, amp_hbm, pos, cnt, pos_hbm, cnt_hbm, fr, fi,
    out_obj, out_probe,
    obj, probe, band_a, band_b, modes, amps, amps_t, right_f, right_b,
    wave, stack, far, near, inten, win, numer, grads, weight, power, illum,
    pos_land, cnt_land, prev_pos, prev_cnt,
    pass_out, pass_in, total, fwd_out, fwd_in, rs_out, rs_in,
    core_out, core_in, plane_sum, plane_in, z_out, zw_out, z_in, zw_in, step_full,
    in_sem, sm_sem, tb_s, tb_r, ag_s, ag_r, fw_s, fw_r, ps_s, ps_r,
    pz_s, pz_r, px_s, px_r, pc_s, pc_r,
    np_s, np_r, nf_s, nf_r, nr_s, nr_r,
    g1_s, g1_r, g2_s, g2_r, gw_s, gw_r, g3_s, g3_r, zw_s, zw_r, g4_s, g4_r, g5_s, g5_r,
):
    R = W // XY
    C = min(32, W)
    s = lax.axis_index("scan")
    t = lax.axis_index("tile")
    core = lax.rem(s, 2)
    zlo = lax.rem(s // 2, 2)
    q = s // 4
    right, left, opp = (lax.rem(t + d, NT) for d in (1, 3, 2))
    other_core = s + 1 - 2 * core
    other_zlo = s + 2 - 4 * zlo
    shard = pl.ds(pl.multiple_of(q * R, R), R)
    has_next = s < NS - 1
    has_prev = s > 0

    def copy_to(src, dst, ssem, rsem, scan, tile):
        return pltpu.make_async_remote_copy(
            src_ref=src, dst_ref=dst, send_sem=ssem, recv_sem=rsem,
            device_id=(scan, tile), device_id_type=MESH,
        )

    def column(step):
        to = lax.rem(q + step, XY)
        return to, to * 4 + zlo * 2 + core

    def all_rows(body):
        for step in range(W // C):
            body(pl.ds(step * C, C))

    def by_rows(body):
        @pl.loop(0, W // C)
        def _(step):
            body(pl.ds(pl.multiple_of(step * C, C), C))

    local = [
        pltpu.make_async_copy(src, dst, in_sem.at[k])
        for k, (src, dst) in enumerate((
            (obj_hbm, obj), (probe_hbm, probe), (amp_hbm.at[t], amps.at[0]), (amp_hbm.at[t + 4], amps.at[1]),
        ))
    ]
    for item in local:
        item.start()

    barrier = pltpu.get_barrier_semaphore()

    def greet(scan, tile):
        pl.semaphore_signal(barrier, inc=1, device_id=(scan, tile), device_id_type=MESH)

    for d in range(1, NT):
        greet(s, lax.rem(t + d, NT))
    for d in range(NT):
        greet(other_zlo, lax.rem(t + d, NT))
    greet(other_core, t)

    @pl.loop(1, XY)
    def _(step):
        greet(column(step)[1], t)

    up_tile = lax.rem(t + jnp.where((core == 0) & (zlo == 1), 1, 0) + jnp.where((core == 0) & (zlo == 0), NT - 1, 0), NT)
    up_tile = jnp.where((core == 0), up_tile, t)
    down_tile = lax.rem(t + jnp.where((core == 1) & (zlo == 0), NT - 1, 0) + jnp.where((core == 1) & (zlo == 1), 1, 0), NT)

    @pl.when(has_next)
    def _():
        greet(s + 1, t)
        greet(s + 1, down_tile)

    @pl.when(has_prev)
    def _():
        greet(s - 1, t)
        greet(s - 1, up_tile)

    local[1].wait()
    modes[0] = probe[...].astype(BF)
    local[0].wait()
    band_a[t] = obj[...].astype(BF)
    pl.semaphore_wait(
        barrier, 2 * NT + XY - 1 + 2 * has_next.astype(jnp.int32) + 2 * has_prev.astype(jnp.int32)
    )

    for d in range(1, NT):
        copy_to(
            modes.at[0, core, :, shard], modes.at[NT - d, core, :, shard],
            pz_s.at[d], pz_r.at[NT - d], s, lax.rem(t + d, NT),
        ).start()

    to_right = [copy_to(band_a.at[t, p], band_a.at[t, p], ag_s.at[p], ag_r.at[p], s, right) for p in (0, 1)]
    to_left = [copy_to(band_a.at[t, p], band_a.at[t, p], ag_s.at[2 + p], ag_r.at[2 + p], s, left) for p in (0, 1)]
    from_left = [copy_to(band_a.at[left, p], band_a.at[left, p], ag_s.at[p], ag_r.at[p], s, right) for p in (0, 1)]
    from_right = [copy_to(band_a.at[right, p], band_a.at[right, p], ag_s.at[2 + p], ag_r.at[2 + p], s, left) for p in (0, 1)]
    on_right = copy_to(band_a.at[left, 0], band_a.at[left, 0], fw_s.at[0], fw_r.at[0], s, right)
    on_left = copy_to(band_a.at[right, 1], band_a.at[right, 1], fw_s.at[1], fw_r.at[1], s, left)
    opp_first = copy_to(band_a.at[opp, 0], band_a.at[opp, 0], fw_s.at[0], fw_r.at[0], s, right)
    opp_second = copy_to(band_a.at[opp, 1], band_a.at[opp, 1], fw_s.at[1], fw_r.at[1], s, left)

    def passed(block, p):
        return copy_to(
            band_a.at[block, p], band_b.at[block, p], ps_s.at[block, p], ps_r.at[block, p],
            s - 1, up_tile if p == 0 else t,
        )

    def start_pass(block, *planes):
        @pl.when(has_prev)
        def _():
            for p in planes:
                passed(block, p).start()

    to_right[0].start()
    to_left[1].start()
    to_right[1].start()
    to_left[0].start()
    start_pass(t, 0, 1)

    tables = [
        copy_to(src, dst, tb_s.at[k], tb_r.at[k], s + 1, t)
        for k, (src, dst) in enumerate(((pos_hbm, pos_land), (cnt_hbm, cnt_land)))
    ]

    @pl.when(has_next)
    def _():
        for item in tables:
            item.start()

    for d in range(1, NT):
        copy_to(
            modes.at[0, core, :, shard], modes.at[d, core, :, shard], pz_s.at[d], pz_r.at[d], s, t
        ).wait_recv()

    def over_columns(step):
        to, device = column(step)
        src = modes.at[pl.ds(1, NT - 1), core, :, shard]
        return copy_to(src, src, px_s.at[to], px_r.at[q], device, t)

    @pl.loop(1, XY)
    def _(step):
        over_columns(step).start()

    from_left[0].wait_recv()
    on_right.start()
    from_right[1].wait_recv()
    on_left.start()
    start_pass(left, 0)
    start_pass(right, 1)
    from_left[1].wait_recv()
    start_pass(left, 1)
    from_right[0].wait_recv()
    start_pass(right, 0)

    for table, ref in ((1.0, right_f), (-1.0, right_b)):
        sign = jnp.asarray(table, BF)
        ref[0:W, 0:W] = fr[...]
        ref[0:W, W:] = fi[...] * sign
        ref[W:, 0:W] = fi[...] * -sign
        ref[W:, W:] = fr[...]
    for u in range(2):
        local[2 + u].wait()
        amps_t[u] = amps[u].astype(F32).T

    opp_first.wait_recv()
    start_pass(opp, 0)
    opp_second.wait_recv()
    start_pass(opp, 1)

    @pl.loop(1, XY)
    def _(step):
        source = lax.rem(q + step, XY)
        rows = pl.ds(pl.multiple_of(source * R, R), R)
        dst = modes.at[pl.ds(1, NT - 1), core, :, rows]
        copy_to(dst, dst, px_s.at[source], px_r.at[source], s, right).wait_recv()

    def to_core(i):
        return copy_to(modes.at[i, core], modes.at[i, core], pc_s.at[i], pc_r.at[i], other_core, t)

    for i in range(1, NT):
        to_core(i).start()

    prev_copies = [
        pltpu.make_async_copy(src, dst, sm_sem.at[k])
        for k, (src, dst) in enumerate(((pos_land, prev_pos), (cnt_land, prev_cnt)))
    ]

    @pl.when(has_prev)
    def _():
        for item, copy in zip(tables, prev_copies):
            item.wait_recv()
            copy.start()

    @pl.when(has_next)
    def _():
        for block in (t, left, right, opp):
            for p in range(2):
                copy_to(
                    band_a.at[block, p], band_b.at[block, p], ps_s.at[block, p], ps_r.at[block, p], s + 1, t
                ).wait_recv()

    row_id = lax.broadcasted_iota(jnp.int32, (W, W), 0)
    col_id = lax.broadcasted_iota(jnp.int32, (W, W), 1)

    def place(slot):
        row, col = pos[slot, 0] - s * W, pos[slot, 1]
        live = jnp.where(slot < cnt[0], 1.0, 0.0).astype(F32)
        return row, lax.rem(col, W), col // W, live

    def place_prev(slot):
        row = jnp.where(has_prev, prev_pos[slot, 0] - (s - 1) * W, 0)
        col = jnp.where(has_prev, prev_pos[slot, 1], 0)
        live = jnp.where(has_prev & (slot < prev_cnt[0]), 1.0, 0.0).astype(F32)
        return row, lax.rem(col, W), col // W, live

    def transform(table, turned):
        for k in range(2):
            half = lax.dot_general(
                turned[...], wave[k], (((1,), (1,)), ((), ())), preferred_element_type=F32
            ).astype(BF)
            stack[k * W : (k + 1) * W, 0:W] = half[0:W]
            stack[k * W : (k + 1) * W, W:] = half[W:]
        return jnp.dot(stack[...], table[...], preferred_element_type=F32)

    def pass_sum(u):
        return copy_to(pass_out.at[u], pass_in.at[u], np_s.at[u], np_r.at[u], s + 1, t)

    last = 2 * NT

    def g1(i):
        planes = pl.ds(2 * i, 2)
        return copy_to(core_out.at[planes], core_in.at[planes], g1_s.at[i], g1_r.at[i], other_core, t)

    g1w = copy_to(core_out.at[last], core_in.at[last], g1_s.at[NT], g1_r.at[NT], other_core, t)

    def shard_of(to):
        return pl.ds(pl.multiple_of(to * R, R), R)

    def g2(i, step):
        to, device = column(step)
        planes = pl.ds(2 * i, 2)
        return copy_to(
            plane_sum.at[planes, shard_of(to)], plane_in.at[q, planes], g2_s.at[i, to], g2_r.at[i, q], device, t
        )

    def g2w(step):
        to, device = column(step)
        return copy_to(plane_sum.at[last, shard_of(to)], plane_in.at[q, last], gw_s.at[to], gw_r.at[q], device, t)

    me_z = 2 * t + zlo

    def g3(i, flip):
        return copy_to(
            z_out.at[i], z_in.at[me_z], g3_s.at[i, flip], g3_r.at[me_z],
            other_zlo if flip else s, lax.rem(t + i, NT),
        )

    def zw(k):
        flip, d = k // NT, lax.rem(k, NT)
        return copy_to(
            zw_out, zw_in.at[me_z], zw_s.at[k], zw_r.at[me_z],
            s + flip * (other_zlo - s), lax.rem(t + d, NT),
        )

    def reduce(i):
        planes = pl.ds(2 * i, 2)

        @pl.loop(1, XY)
        def _(step):
            source = lax.rem(q + step, XY)
            copy_to(
                plane_sum.at[planes, shard], plane_in.at[source, planes],
                g2_s.at[i, source], g2_r.at[i, source], s, right,
            ).wait_recv()

        plane_in[q, planes] = plane_sum[planes, shard]
        for p in range(2):
            value = plane_in[0, 2 * i + p].astype(F32)
            for source in range(1, XY):
                value = value + plane_in[source, 2 * i + p].astype(F32)
            z_out[i, p] = value.astype(BF)
        g3(i, 1).start()

        @pl.when(i > 0)
        def _():
            g3(i, 0).start()

        @pl.when(i == 0)
        def _():
            z_in[me_z] = z_out[0]

    def reduce_weight():
        @pl.loop(1, XY)
        def _(step):
            source = lax.rem(q + step, XY)
            copy_to(plane_sum.at[last, shard], plane_in.at[source, last], gw_s.at[source], gw_r.at[source], s, right).wait_recv()

        plane_in[q, last] = plane_sum[last, shard]
        value = plane_in[0, last].astype(F32)
        for source in range(1, XY):
            value = value + plane_in[source, last].astype(F32)
        zw_out[...] = value.astype(BF)
        zw_in[me_z] = zw_out[...]

        @pl.loop(1, 2 * NT)
        def _(k):
            zw(k).start()

    for u in range(2):
        row, lane, block, live = place(t + 4 * u)
        after = jnp.minimum(block + 1, NT - 1)
        for p in range(2):
            upper = jnp.where(col_id >= lane, band_a[block, p].astype(F32), band_a[after, p].astype(F32))
            lower = jnp.where(col_id >= lane, band_b[block, p].astype(F32), band_b[after, p].astype(F32))
            merged = jnp.where(row_id >= row, upper, lower)
            merged = pltpu.roll(merged, lax.rem(W - row, W), 0)
            win[p] = pltpu.roll(merged, lax.rem(W - lane, W), 1)

        def start_slot(rows):
            square = live * (win[0, rows] * win[0, rows] + win[1, rows] * win[1, rows])
            if u == 0:
                weight[rows] = square
            else:
                weight[rows] += square
                core_out[last, rows] = weight[rows].astype(BF)
            inten[rows] = jnp.zeros((C, W), F32)
            for p in range(2):
                numer[u, p, rows] = jnp.zeros((C, W), F32)

        by_rows(start_slot)
        if u == 1:
            g1w.start()

        @pl.loop(0, NT)
        def _(i):
            if u == 0:
                @pl.when(i > 0)
                def _():
                    copy_to(modes.at[i, 1 - core], modes.at[i, 1 - core], pc_s.at[i], pc_r.at[i], other_core, t).wait_recv()

            def exit_rows(rows):
                wr, wi = win[0, rows], win[1, rows]
                square = 0.0
                for cc in range(2):
                    pr = modes[i, cc, 0, rows].astype(F32)
                    pi = modes[i, cc, 1, rows].astype(F32)
                    wave[cc, rows, 0:W] = (pr * wr - pi * wi).astype(BF)
                    wave[cc, rows, W:] = (pr * wi + pi * wr).astype(BF)
                    square = square + (pr * pr + pi * pi)
                if u == 0:
                    power[rows] = jnp.where(i == 0, 0.0, power[rows]) + square

            all_rows(exit_rows)
            far[i] = transform(right_f, right_b)

            def add_rows(rows):
                value = inten[rows]
                for cc in range(2):
                    both = pl.ds(rows.start + cc * W, C)
                    fa, fb = far[i, both, 0:W], far[i, both, W:]
                    value = value + (fa * fa + fb * fb)
                inten[rows] = value

            all_rows(add_rows)

        def factor_rows(rows):
            size = jnp.maximum(jnp.sqrt(inten[rows]), amp_floor)
            inten[rows] = live * (amps_t[u, rows] / size - 1.0)

        by_rows(factor_rows)

        if u == 1:
            g1w.wait_recv()

            def weight_rows(rows):
                plane_sum[last, rows] = (weight[rows] + core_in[last, rows].astype(F32)).astype(BF)

            by_rows(weight_rows)

            @pl.loop(1, XY)
            def _(step):
                g2w(step).start()

        def finish(i):
            g1(i).wait_recv()

            def sum_rows(rows):
                for p in range(2):
                    k = 2 * i + p
                    plane_sum[k, rows] = (grads[i, core, p, rows] + core_in[k, rows].astype(F32)).astype(BF)

            by_rows(sum_rows)

            @pl.loop(1, XY)
            def _(step):
                g2(i, step).start()

        @pl.loop(0, NT)
        def _(i):
            turns = (1 - core, core)

            def change_rows(rows):
                factor = inten[rows]
                for turn, cc in enumerate(turns):
                    both = pl.ds(rows.start + pl.multiple_of(cc * W, W), C)
                    wave[turn, rows, 0:W] = (factor * far[i, both, 0:W]).astype(BF)
                    wave[turn, rows, W:] = (factor * far[i, both, W:]).astype(BF)

            all_rows(change_rows)
            near[...] = transform(right_b, right_f)

            for turn, cc in enumerate(turns):
                def near_rows(rows):
                    both = pl.ds(rows.start + turn * W, C)
                    pr = modes[i, cc, 0, rows].astype(F32)
                    pi = modes[i, cc, 1, rows].astype(F32)
                    wr, wi = win[0, rows], win[1, rows]
                    nr, ni = near[both, 0:W], near[both, W:]
                    numer[u, 0, rows] += pr * nr + pi * ni
                    numer[u, 1, rows] += pr * ni - pi * nr
                    step = (wr * nr + wi * ni, wr * ni - wi * nr)
                    for p in range(2):
                        if u == 0:
                            grads[i, cc, p, rows] = step[p]
                        elif turn == 0:
                            core_out[2 * i + p, rows] = (grads[i, cc, p, rows] + step[p]).astype(BF)
                        else:
                            grads[i, cc, p, rows] += step[p]

                all_rows(near_rows)
                if u == 1 and turn == 0:
                    g1(i).start()

                    @pl.when(i > 0)
                    def _():
                        finish(i - 1)

            if u == 1:
                @pl.when(i == NT - 2)
                def _():
                    reduce_weight()

                @pl.when(i > 1)
                def _():
                    reduce(i - 2)

        for p in range(2):
            rolled = pltpu.roll(numer[u, p], lane, 1)
            rolled = pltpu.roll(rolled, row, 0)
            numer[u, p] = rolled
            pass_out[u, p] = rolled.astype(BF)

        @pl.when(has_next)
        def _():
            pass_sum(u).start()

    finish(NT - 1)
    reduce(NT - 2)

    @pl.when(has_prev)
    def _():
        for item in prev_copies:
            item.wait()

    def illuminate(where_is, upper):
        @pl.loop(0, 8)
        def _(slot):
            row, lane, block, live = where_is(slot)
            moved = pltpu.roll(pltpu.roll(power[...], lane, 1), row, 0)
            cols = jnp.where(col_id >= lane, block, block + 1) == t
            rows = (row_id >= row) if upper else (row_id < row)
            illum[...] += live * jnp.where(cols & rows, moved, 0.0)

    illum[...] = jnp.zeros((W, W), F32)
    illuminate(place, True)

    @pl.when(has_prev)
    def _():
        for u in range(2):
            copy_to(pass_out.at[u], pass_in.at[u], np_s.at[u], np_r.at[u], s - 1, t).wait_recv()

    order = (opp, right, left, t)
    spots = [place(t + 4 * u) for u in range(2)] + [place_prev(t + 4 * u) for u in range(2)]

    def total_rows(rows):
        start = rows.start
        row_at = lax.broadcasted_iota(jnp.int32, (C, W), 0) + start
        col_at = lax.broadcasted_iota(jnp.int32, (C, W), 1)
        owners = [jnp.where(col_at >= lane, first, first + 1) for _, lane, first, _ in spots]
        for p in range(2):
            values = [numer[u, p, rows] for u in range(2)] + [pass_in[u, p, rows].astype(F32) for u in range(2)]
            values = [
                jnp.where(row_at >= spot[0] if k < 2 else row_at < spot[0], value, 0.0)
                for k, (value, spot) in enumerate(zip(values, spots))
            ]
            for slot, block in enumerate(order):
                value = 0.0
                for k in range(4):
                    value = value + jnp.where(owners[k] == block, values[k], 0.0)
                if slot == 0:
                    fwd_out[p, rows] = value.astype(BF)
                elif slot == 3:
                    total[2, p, rows] = value
                elif p == 2 - slot:
                    rs_out[slot - 1, p, rows] = value.astype(BF)
                else:
                    total[slot - 1, 0, rows] = value

    by_rows(total_rows)
    forwards = []
    for p, to in ((0, right), (1, left)):
        item = copy_to(fwd_out.at[p], fwd_in.at[p], nf_s.at[p], nf_r.at[p], s, to)
        item.start()
        forwards.append(item)
    sends = {}
    for way, to in ((0, right), (1, left)):
        for p in range(2):
            sends[way, p] = copy_to(
                rs_out.at[way, p], rs_in.at[way, p], nr_s.at[way, p], nr_r.at[way, p], s, to
            )
    sends[0, 1].start()
    sends[1, 0].start()
    reduce(NT - 1)
    illuminate(place_prev, False)
    for way in range(2):
        forwards[way].wait_recv()
        rs_out[way, way] = (total[way, 0] + fwd_in[way].astype(F32)).astype(BF)
        sends[way, way].start()

    for flip in range(2):
        for d in range(NT):
            if flip == 0 and d == 0:
                continue
            source = 2 * lax.rem(t + d, NT) + (1 - zlo if flip else zlo)
            copy_to(z_out.at[d], z_in.at[source], g3_s.at[d, 0], g3_r.at[source], s, right).wait_recv()
            copy_to(zw_out, zw_in.at[source], zw_s.at[d], zw_r.at[source], s, right).wait_recv()
    parts = [[z_in[k, 0], z_in[k, 1], zw_in[k]] for k in range(2 * NT)]
    summed = [item.astype(F32) for item in parts[0]]
    for part in parts[1:]:
        summed = [value + item.astype(F32) for value, item in zip(summed, part)]
    for p in range(2):
        step_full[core, p, shard] = summed[p] / (summed[2] + damping)

    def g4(step):
        to, device = column(step)
        src = step_full.at[core, :, shard]
        return copy_to(src, src, g4_s.at[to], g4_r.at[q], device, t)

    @pl.loop(1, XY)
    def _(step):
        g4(step).start()

    @pl.loop(1, XY)
    def _(step):
        source = lax.rem(q + step, XY)
        dst = step_full.at[core, :, shard_of(source)]
        copy_to(dst, dst, g4_s.at[source], g4_r.at[source], s, right).wait_recv()

    g5 = copy_to(step_full.at[core], step_full.at[core], g5_s, g5_r, other_core, t)
    g5.start()

    for item in sends.values():
        item.wait_recv()

    def object_rows(rows):
        scale = illum[rows] + damping
        for p in range(2):
            value = total[2, p, rows] + (rs_in[0, p, rows].astype(F32) + rs_in[1, p, rows].astype(F32))
            out_obj[p, rows] = obj[p, rows] + value / scale

    by_rows(object_rows)
    copy_to(step_full.at[1 - core], step_full.at[1 - core], g5_s, g5_r, other_core, t).wait_recv()
    out_probe[...] = step_full[...]

    for item in to_right + to_left + [on_right, on_left, g1w, g5] + forwards + list(sends.values()):
        item.wait_send()
    for d in range(1, NT):
        copy_to(
            modes.at[0, core, :, shard], modes.at[NT - d, core, :, shard],
            pz_s.at[d], pz_r.at[NT - d], s, lax.rem(t + d, NT),
        ).wait_send()
        to_core(d).wait_send()

    for i in range(NT):
        g3(i, 1).wait_send()
        if i > 0:
            g3(i, 0).wait_send()

    @pl.loop(1, 2 * NT)
    def _(k):
        zw(k).wait_send()

    @pl.loop(0, NT)
    def _(i):
        g1(i).wait_send()

    @pl.loop(1, XY)
    def _(step):
        over_columns(step).wait_send()
        g2w(step).wait_send()
        g4(step).wait_send()

        @pl.loop(0, NT)
        def _(i):
            g2(i, step).wait_send()

    @pl.when(has_prev)
    def _():
        for block in (t, left, right, opp):
            for p in range(2):
                passed(block, p).wait_send()

    @pl.when(has_next)
    def _():
        for item in tables:
            item.wait_send()
        for u in range(2):
            pass_sum(u).wait_send()


def shards(NS, NT, object_field, probe_modes, amplitudes, positions, counts):
    W = amplitudes.shape[1]
    XY = NS // 4
    R = W // XY
    fr, fi = dft_tables(W)
    vmem = pl.BlockSpec(memory_space=pltpu.VMEM)
    smem = pl.BlockSpec(memory_space=pltpu.SMEM)
    hbm = pl.BlockSpec(memory_space=pl.ANY)
    dma = pltpu.SemaphoreType.DMA

    def buf(*shape, dtype=F32):
        return pltpu.VMEM(shape, dtype)

    scratch = [
        buf(2, W, W), buf(2, 2, W, W),
        buf(NT, 2, W, W, dtype=BF), buf(NT, 2, W, W, dtype=BF), buf(NT, 2, 2, W, W, dtype=BF),
        buf(2, W, W, dtype=BF), buf(2, W, W), buf(2 * W, 2 * W, dtype=BF), buf(2 * W, 2 * W, dtype=BF),
        buf(2, W, 2 * W, dtype=BF), buf(2 * W, 2 * W, dtype=BF), buf(NT, 2 * W, 2 * W), buf(2 * W, 2 * W),
        buf(W, W), buf(2, W, W), buf(2, 2, W, W), buf(NT, 2, 2, W, W), buf(W, W), buf(W, W), buf(W, W),
        buf(8, 2, dtype=jnp.int32), buf(1, dtype=jnp.int32),
        pltpu.SMEM((8, 2), jnp.int32), pltpu.SMEM((1,), jnp.int32),
        buf(2, 2, W, W, dtype=BF), buf(2, 2, W, W, dtype=BF), buf(3, 2, W, W),
        buf(2, W, W, dtype=BF), buf(2, W, W, dtype=BF), buf(2, 2, W, W, dtype=BF), buf(2, 2, W, W, dtype=BF),
        buf(2 * NT + 1, W, W, dtype=BF), buf(2 * NT + 1, W, W, dtype=BF), buf(2 * NT + 1, W, W, dtype=BF),
        buf(XY, 2 * NT + 1, R, W, dtype=BF), buf(NT, 2, R, W, dtype=BF), buf(R, W, dtype=BF), buf(2 * NT, 2, R, W, dtype=BF), buf(2 * NT, R, W, dtype=BF),
        buf(2, 2, W, W),
        dma((4,)), dma((2,)), dma((2,)), dma((2,)), dma((4,)), dma((4,)), dma((2,)), dma((2,)), dma((4, 2)), dma((4, 2)),
        dma((NT,)), dma((NT,)), dma((XY,)), dma((XY,)), dma((NT,)), dma((NT,)),
        dma((2,)), dma((2,)), dma((2,)), dma((2,)), dma((2, 2)), dma((2, 2)),
        dma((NT + 1,)), dma((NT + 1,)), dma((NT, XY)), dma((NT, XY)), dma((XY,)), dma((XY,)),
        dma((NT, 2)), dma((2 * NT,)), dma((2 * NT,)), dma((2 * NT,)), dma((XY,)), dma((XY,)), dma, dma,
    ]
    new_object, probe_step = pl.pallas_call(
        functools.partial(kernel, W, XY, NS, NT),
        out_shape=(
            jax.ShapeDtypeStruct(object_field.shape, F32),
            jax.ShapeDtypeStruct(probe_modes.shape, F32),
        ),
        in_specs=[hbm, hbm, hbm, smem, smem, vmem, vmem, vmem, vmem],
        out_specs=(vmem, vmem),
        scratch_shapes=scratch,
        compiler_params=pltpu.CompilerParams(
            collective_id=0, has_side_effects=True, vmem_limit_bytes=58 * 1024 * 1024
        ),
    )(object_field, probe_modes, amplitudes, positions, counts, positions, counts, jnp.asarray(fr), jnp.asarray(fi))
    return new_object, probe_step


def solution(mesh):
    placed = (
        P(None, "scan", "tile"),
        P("tile", None, None, None),
        P("scan", None, None),
        P("scan", None),
        P("scan"),
    )
    return jax.shard_map(
        functools.partial(shards, mesh.shape["scan"], mesh.shape["tile"]),
        mesh=mesh,
        in_specs=placed,
        out_specs=(P(None, "scan", "tile"), P("tile", None, None, None)),
        check_vma=False,
    )
```

```python
import functools
import math

import jax
import jax.numpy as jnp
import numpy as np
from jax import lax
from jax.experimental import pallas as pl
from jax.experimental.pallas import tpu as pltpu
from jax.sharding import PartitionSpec as P

damping = 1.0
amp_floor = 0.5
MESH = pl.DeviceIdType.MESH
BF = jnp.bfloat16
F32 = jnp.float32


def dft_tables(width):
    index = np.arange(width)
    angle = (index[:, None] * index[None, :] % width) * (2.0 * math.pi / width)
    scale = 1.0 / math.sqrt(width)
    return (np.cos(angle) * scale).astype(BF), (-np.sin(angle) * scale).astype(BF)


def kernel(
    W, XY, NS, NT,
    obj_hbm, probe_hbm, amp_hbm, pos, cnt, pos_hbm, cnt_hbm, fr, fi,
    out_obj, out_probe,
    obj, probe, band_a, band_b, modes, amps, amps_t, right_f, right_b,
    wave, stack, far, near, inten, win, numer, grads, weight, power, illum,
    pos_land, cnt_land, prev_pos, prev_cnt,
    pass_out, pass_in, total, fwd_out, fwd_in, rs_out, rs_in,
    core_out, core_in, plane_sum, plane_in, z_out, zw_out, z_in, zw_in, step_full,
    in_sem, sm_sem, tb_s, tb_r, ag_s, ag_r, fw_s, fw_r, ps_s, ps_r,
    pz_s, pz_r, px_s, px_r, pc_s, pc_r,
    np_s, np_r, nf_s, nf_r, nr_s, nr_r,
    g1_s, g1_r, g2_s, g2_r, gw_s, gw_r, g3_s, g3_r, zw_s, zw_r, g4_s, g4_r, g5_s, g5_r,
):
    R = W // XY
    C = min(32, W)
    s = lax.axis_index("scan")
    t = lax.axis_index("tile")
    core = lax.rem(s, 2)
    zlo = lax.rem(s // 2, 2)
    q = s // 4
    right, left, opp = (lax.rem(t + d, NT) for d in (1, 3, 2))
    other_core = s + 1 - 2 * core
    other_zlo = s + 2 - 4 * zlo
    shard = pl.ds(pl.multiple_of(q * R, R), R)
    has_next = s < NS - 1
    has_prev = s > 0

    def copy_to(src, dst, ssem, rsem, scan, tile):
        return pltpu.make_async_remote_copy(
            src_ref=src, dst_ref=dst, send_sem=ssem, recv_sem=rsem,
            device_id=(scan, tile), device_id_type=MESH,
        )

    def column(step):
        to = lax.rem(q + step, XY)
        return to, to * 4 + zlo * 2 + core

    def all_rows(body):
        for step in range(W // C):
            body(pl.ds(step * C, C))

    def by_rows(body):
        @pl.loop(0, W // C)
        def _(step):
            body(pl.ds(pl.multiple_of(step * C, C), C))

    local = [
        pltpu.make_async_copy(src, dst, in_sem.at[k])
        for k, (src, dst) in enumerate((
            (obj_hbm, obj), (probe_hbm, probe), (amp_hbm.at[t], amps.at[0]), (amp_hbm.at[t + 4], amps.at[1]),
        ))
    ]
    for item in local:
        item.start()

    barrier = pltpu.get_barrier_semaphore()

    def greet(scan, tile):
        pl.semaphore_signal(barrier, inc=1, device_id=(scan, tile), device_id_type=MESH)

    for d in range(1, NT):
        greet(s, lax.rem(t + d, NT))
    for d in range(NT):
        greet(other_zlo, lax.rem(t + d, NT))
    greet(other_core, t)

    @pl.loop(1, XY)
    def _(step):
        greet(column(step)[1], t)

    up_tile = lax.rem(t + jnp.where((core == 0) & (zlo == 1), 1, 0) + jnp.where((core == 0) & (zlo == 0), NT - 1, 0), NT)
    up_tile = jnp.where((core == 0), up_tile, t)
    down_tile = lax.rem(t + jnp.where((core == 1) & (zlo == 0), NT - 1, 0) + jnp.where((core == 1) & (zlo == 1), 1, 0), NT)

    @pl.when(has_next)
    def _():
        greet(s + 1, t)
        greet(s + 1, down_tile)

    @pl.when(has_prev)
    def _():
        greet(s - 1, t)
        greet(s - 1, up_tile)

    local[1].wait()
    modes[0] = probe[...].astype(BF)
    local[0].wait()
    band_a[t] = obj[...].astype(BF)
    pl.semaphore_wait(
        barrier, 2 * NT + XY - 1 + 2 * has_next.astype(jnp.int32) + 2 * has_prev.astype(jnp.int32)
    )

    for d in range(1, NT):
        copy_to(
            modes.at[0, core, :, shard], modes.at[NT - d, core, :, shard],
            pz_s.at[d], pz_r.at[NT - d], s, lax.rem(t + d, NT),
        ).start()

    to_right = [copy_to(band_a.at[t, p], band_a.at[t, p], ag_s.at[p], ag_r.at[p], s, right) for p in (0, 1)]
    to_left = [copy_to(band_a.at[t, p], band_a.at[t, p], ag_s.at[2 + p], ag_r.at[2 + p], s, left) for p in (0, 1)]
    from_left = [copy_to(band_a.at[left, p], band_a.at[left, p], ag_s.at[p], ag_r.at[p], s, right) for p in (0, 1)]
    from_right = [copy_to(band_a.at[right, p], band_a.at[right, p], ag_s.at[2 + p], ag_r.at[2 + p], s, left) for p in (0, 1)]
    on_right = copy_to(band_a.at[left, 0], band_a.at[left, 0], fw_s.at[0], fw_r.at[0], s, right)
    on_left = copy_to(band_a.at[right, 1], band_a.at[right, 1], fw_s.at[1], fw_r.at[1], s, left)
    opp_first = copy_to(band_a.at[opp, 0], band_a.at[opp, 0], fw_s.at[0], fw_r.at[0], s, right)
    opp_second = copy_to(band_a.at[opp, 1], band_a.at[opp, 1], fw_s.at[1], fw_r.at[1], s, left)

    def passed(block, p):
        return copy_to(
            band_a.at[block, p], band_b.at[block, p], ps_s.at[block, p], ps_r.at[block, p],
            s - 1, up_tile if p == 0 else t,
        )

    def start_pass(block, *planes):
        @pl.when(has_prev)
        def _():
            for p in planes:
                passed(block, p).start()

    to_right[0].start()
    to_left[1].start()
    to_right[1].start()
    to_left[0].start()
    start_pass(t, 0, 1)

    tables = [
        copy_to(src, dst, tb_s.at[k], tb_r.at[k], s + 1, t)
        for k, (src, dst) in enumerate(((pos_hbm, pos_land), (cnt_hbm, cnt_land)))
    ]

    @pl.when(has_next)
    def _():
        for item in tables:
            item.start()

    for d in range(1, NT):
        copy_to(
            modes.at[0, core, :, shard], modes.at[d, core, :, shard], pz_s.at[d], pz_r.at[d], s, t
        ).wait_recv()

    def over_columns(step):
        to, device = column(step)
        src = modes.at[pl.ds(1, NT - 1), core, :, shard]
        return copy_to(src, src, px_s.at[to], px_r.at[q], device, t)

    @pl.loop(1, XY)
    def _(step):
        over_columns(step).start()

    from_left[0].wait_recv()
    on_right.start()
    from_right[1].wait_recv()
    on_left.start()
    start_pass(left, 0)
    start_pass(right, 1)
    from_left[1].wait_recv()
    start_pass(left, 1)
    from_right[0].wait_recv()
    start_pass(right, 0)

    for table, ref in ((1.0, right_f), (-1.0, right_b)):
        sign = jnp.asarray(table, BF)
        ref[0:W, 0:W] = fr[...]
        ref[0:W, W:] = fi[...] * sign
        ref[W:, 0:W] = fi[...] * -sign
        ref[W:, W:] = fr[...]
    for u in range(2):
        local[2 + u].wait()
        amps_t[u] = amps[u].astype(F32).T

    opp_first.wait_recv()
    start_pass(opp, 0)
    opp_second.wait_recv()
    start_pass(opp, 1)

    @pl.loop(1, XY)
    def _(step):
        source = lax.rem(q + step, XY)
        rows = pl.ds(pl.multiple_of(source * R, R), R)
        dst = modes.at[pl.ds(1, NT - 1), core, :, rows]
        copy_to(dst, dst, px_s.at[source], px_r.at[source], s, right).wait_recv()

    def to_core(i):
        return copy_to(modes.at[i, core], modes.at[i, core], pc_s.at[i], pc_r.at[i], other_core, t)

    for i in range(1, NT):
        to_core(i).start()

    prev_copies = [
        pltpu.make_async_copy(src, dst, sm_sem.at[k])
        for k, (src, dst) in enumerate(((pos_land, prev_pos), (cnt_land, prev_cnt)))
    ]

    @pl.when(has_prev)
    def _():
        for item, copy in zip(tables, prev_copies):
            item.wait_recv()
            copy.start()

    @pl.when(has_next)
    def _():
        for block in (t, left, right, opp):
            for p in range(2):
                copy_to(
                    band_a.at[block, p], band_b.at[block, p], ps_s.at[block, p], ps_r.at[block, p], s + 1, t
                ).wait_recv()

    row_id = lax.broadcasted_iota(jnp.int32, (W, W), 0)
    col_id = lax.broadcasted_iota(jnp.int32, (W, W), 1)

    def place(slot):
        row, col = pos[slot, 0] - s * W, pos[slot, 1]
        live = jnp.where(slot < cnt[0], 1.0, 0.0).astype(F32)
        return row, lax.rem(col, W), col // W, live

    def place_prev(slot):
        row = jnp.where(has_prev, prev_pos[slot, 0] - (s - 1) * W, 0)
        col = jnp.where(has_prev, prev_pos[slot, 1], 0)
        live = jnp.where(has_prev & (slot < prev_cnt[0]), 1.0, 0.0).astype(F32)
        return row, lax.rem(col, W), col // W, live

    def transform(table, turned):
        for k in range(2):
            half = lax.dot_general(
                turned[...], wave[k], (((1,), (1,)), ((), ())), preferred_element_type=F32
            ).astype(BF)
            stack[k * W : (k + 1) * W, 0:W] = half[0:W]
            stack[k * W : (k + 1) * W, W:] = half[W:]
        return jnp.dot(stack[...], table[...], preferred_element_type=F32)

    def pass_sum(u):
        return copy_to(pass_out.at[u], pass_in.at[u], np_s.at[u], np_r.at[u], s + 1, t)

    last = 2 * NT

    def g1(i):
        planes = pl.ds(2 * i, 2)
        return copy_to(core_out.at[planes], core_in.at[planes], g1_s.at[i], g1_r.at[i], other_core, t)

    g1w = copy_to(core_out.at[last], core_in.at[last], g1_s.at[NT], g1_r.at[NT], other_core, t)

    def shard_of(to):
        return pl.ds(pl.multiple_of(to * R, R), R)

    def g2(i, step):
        to, device = column(step)
        planes = pl.ds(2 * i, 2)
        return copy_to(
            plane_sum.at[planes, shard_of(to)], plane_in.at[q, planes], g2_s.at[i, to], g2_r.at[i, q], device, t
        )

    def g2w(step):
        to, device = column(step)
        return copy_to(plane_sum.at[last, shard_of(to)], plane_in.at[q, last], gw_s.at[to], gw_r.at[q], device, t)

    me_z = 2 * t + zlo

    def g3(i, flip):
        return copy_to(
            z_out.at[i], z_in.at[me_z], g3_s.at[i, flip], g3_r.at[me_z],
            other_zlo if flip else s, lax.rem(t + i, NT),
        )

    def zw(k):
        flip, d = k // NT, lax.rem(k, NT)
        return copy_to(
            zw_out, zw_in.at[me_z], zw_s.at[k], zw_r.at[me_z],
            s + flip * (other_zlo - s), lax.rem(t + d, NT),
        )

    def reduce(i):
        planes = pl.ds(2 * i, 2)

        @pl.loop(1, XY)
        def _(step):
            source = lax.rem(q + step, XY)
            copy_to(
                plane_sum.at[planes, shard], plane_in.at[source, planes],
                g2_s.at[i, source], g2_r.at[i, source], s, right,
            ).wait_recv()

        plane_in[q, planes] = plane_sum[planes, shard]
        for p in range(2):
            value = plane_in[0, 2 * i + p].astype(F32)
            for source in range(1, XY):
                value = value + plane_in[source, 2 * i + p].astype(F32)
            z_out[i, p] = value.astype(BF)
        g3(i, 1).start()

        @pl.when(i > 0)
        def _():
            g3(i, 0).start()

        @pl.when(i == 0)
        def _():
            z_in[me_z] = z_out[0]

    def reduce_weight():
        @pl.loop(1, XY)
        def _(step):
            source = lax.rem(q + step, XY)
            copy_to(plane_sum.at[last, shard], plane_in.at[source, last], gw_s.at[source], gw_r.at[source], s, right).wait_recv()

        plane_in[q, last] = plane_sum[last, shard]
        value = plane_in[0, last].astype(F32)
        for source in range(1, XY):
            value = value + plane_in[source, last].astype(F32)
        zw_out[...] = value.astype(BF)
        zw_in[me_z] = zw_out[...]

        @pl.loop(1, 2 * NT)
        def _(k):
            zw(k).start()

    for u in range(2):
        row, lane, block, live = place(t + 4 * u)
        after = jnp.minimum(block + 1, NT - 1)
        for p in range(2):
            upper = jnp.where(col_id >= lane, band_a[block, p].astype(F32), band_a[after, p].astype(F32))
            lower = jnp.where(col_id >= lane, band_b[block, p].astype(F32), band_b[after, p].astype(F32))
            merged = jnp.where(row_id >= row, upper, lower)
            merged = pltpu.roll(merged, lax.rem(W - row, W), 0)
            win[p] = pltpu.roll(merged, lax.rem(W - lane, W), 1)

        def start_slot(rows):
            square = live * (win[0, rows] * win[0, rows] + win[1, rows] * win[1, rows])
            if u == 0:
                weight[rows] = square
            else:
                weight[rows] += square
                core_out[last, rows] = weight[rows].astype(BF)
            inten[rows] = jnp.zeros((C, W), F32)
            for p in range(2):
                numer[u, p, rows] = jnp.zeros((C, W), F32)

        by_rows(start_slot)
        if u == 1:
            g1w.start()

        @pl.loop(0, NT)
        def _(i):
            if u == 0:
                @pl.when(i > 0)
                def _():
                    copy_to(modes.at[i, 1 - core], modes.at[i, 1 - core], pc_s.at[i], pc_r.at[i], other_core, t).wait_recv()

            def exit_rows(rows):
                wr, wi = win[0, rows], win[1, rows]
                square = 0.0
                for cc in range(2):
                    pr = modes[i, cc, 0, rows].astype(F32)
                    pi = modes[i, cc, 1, rows].astype(F32)
                    wave[cc, rows, 0:W] = (pr * wr - pi * wi).astype(BF)
                    wave[cc, rows, W:] = (pr * wi + pi * wr).astype(BF)
                    square = square + (pr * pr + pi * pi)
                if u == 0:
                    power[rows] = jnp.where(i == 0, 0.0, power[rows]) + square

            all_rows(exit_rows)
            far[i] = transform(right_f, right_b)

            def add_rows(rows):
                value = inten[rows]
                for cc in range(2):
                    both = pl.ds(rows.start + cc * W, C)
                    fa, fb = far[i, both, 0:W], far[i, both, W:]
                    value = value + (fa * fa + fb * fb)
                inten[rows] = value

            all_rows(add_rows)

        def factor_rows(rows):
            size = jnp.maximum(jnp.sqrt(inten[rows]), amp_floor)
            inten[rows] = live * (amps_t[u, rows] / size - 1.0)

        by_rows(factor_rows)

        if u == 1:
            g1w.wait_recv()

            def weight_rows(rows):
                plane_sum[last, rows] = (weight[rows] + core_in[last, rows].astype(F32)).astype(BF)

            by_rows(weight_rows)

            @pl.loop(1, XY)
            def _(step):
                g2w(step).start()

        def finish(i):
            g1(i).wait_recv()

            def sum_rows(rows):
                for p in range(2):
                    k = 2 * i + p
                    plane_sum[k, rows] = (grads[i, core, p, rows] + core_in[k, rows].astype(F32)).astype(BF)

            by_rows(sum_rows)

            @pl.loop(1, XY)
            def _(step):
                g2(i, step).start()

        @pl.loop(0, NT)
        def _(i):
            turns = (1 - core, core)

            def change_rows(rows):
                factor = inten[rows]
                for turn, cc in enumerate(turns):
                    both = pl.ds(rows.start + pl.multiple_of(cc * W, W), C)
                    wave[turn, rows, 0:W] = (factor * far[i, both, 0:W]).astype(BF)
                    wave[turn, rows, W:] = (factor * far[i, both, W:]).astype(BF)

            all_rows(change_rows)
            near[...] = transform(right_b, right_f)

            for turn, cc in enumerate(turns):
                def near_rows(rows):
                    both = pl.ds(rows.start + turn * W, C)
                    pr = modes[i, cc, 0, rows].astype(F32)
                    pi = modes[i, cc, 1, rows].astype(F32)
                    wr, wi = win[0, rows], win[1, rows]
                    nr, ni = near[both, 0:W], near[both, W:]
                    numer[u, 0, rows] += pr * nr + pi * ni
                    numer[u, 1, rows] += pr * ni - pi * nr
                    step = (wr * nr + wi * ni, wr * ni - wi * nr)
                    for p in range(2):
                        if u == 0:
                            grads[i, cc, p, rows] = step[p]
                        elif turn == 0:
                            core_out[2 * i + p, rows] = (grads[i, cc, p, rows] + step[p]).astype(BF)
                        else:
                            grads[i, cc, p, rows] += step[p]

                all_rows(near_rows)
                if u == 1 and turn == 0:
                    g1(i).start()

                    @pl.when(i > 0)
                    def _():
                        finish(i - 1)


        for p in range(2):
            rolled = pltpu.roll(numer[u, p], lane, 1)
            rolled = pltpu.roll(rolled, row, 0)
            numer[u, p] = rolled
            pass_out[u, p] = rolled.astype(BF)

        @pl.when(has_next)
        def _():
            pass_sum(u).start()

    finish(NT - 1)

    @pl.when(has_prev)
    def _():
        for item in prev_copies:
            item.wait()

    def illuminate(where_is, upper):
        @pl.loop(0, 8)
        def _(slot):
            row, lane, block, live = where_is(slot)
            moved = pltpu.roll(pltpu.roll(power[...], lane, 1), row, 0)
            cols = jnp.where(col_id >= lane, block, block + 1) == t
            rows = (row_id >= row) if upper else (row_id < row)
            illum[...] += live * jnp.where(cols & rows, moved, 0.0)

    illum[...] = jnp.zeros((W, W), F32)

    @pl.when(has_prev)
    def _():
        for u in range(2):
            copy_to(pass_out.at[u], pass_in.at[u], np_s.at[u], np_r.at[u], s - 1, t).wait_recv()

    order = (opp, right, left, t)
    spots = [place(t + 4 * u) for u in range(2)] + [place_prev(t + 4 * u) for u in range(2)]

    def total_rows(rows):
        start = rows.start
        row_at = lax.broadcasted_iota(jnp.int32, (C, W), 0) + start
        col_at = lax.broadcasted_iota(jnp.int32, (C, W), 1)
        owners = [jnp.where(col_at >= lane, first, first + 1) for _, lane, first, _ in spots]
        for p in range(2):
            values = [numer[u, p, rows] for u in range(2)] + [pass_in[u, p, rows].astype(F32) for u in range(2)]
            values = [
                jnp.where(row_at >= spot[0] if k < 2 else row_at < spot[0], value, 0.0)
                for k, (value, spot) in enumerate(zip(values, spots))
            ]
            for slot, block in enumerate(order):
                value = 0.0
                for k in range(4):
                    value = value + jnp.where(owners[k] == block, values[k], 0.0)
                if slot == 0:
                    fwd_out[p, rows] = value.astype(BF)
                elif slot == 3:
                    total[2, p, rows] = value
                elif p == 2 - slot:
                    rs_out[slot - 1, p, rows] = value.astype(BF)
                else:
                    total[slot - 1, 0, rows] = value

    by_rows(total_rows)
    forwards = []
    for p, to in ((0, right), (1, left)):
        item = copy_to(fwd_out.at[p], fwd_in.at[p], nf_s.at[p], nf_r.at[p], s, to)
        item.start()
        forwards.append(item)
    sends = {}
    for way, to in ((0, right), (1, left)):
        for p in range(2):
            sends[way, p] = copy_to(
                rs_out.at[way, p], rs_in.at[way, p], nr_s.at[way, p], nr_r.at[way, p], s, to
            )
    sends[0, 1].start()
    sends[1, 0].start()
    reduce_weight()
    for i in range(NT):
        reduce(i)
    illuminate(place, True)
    illuminate(place_prev, False)
    for way in range(2):
        forwards[way].wait_recv()
        rs_out[way, way] = (total[way, 0] + fwd_in[way].astype(F32)).astype(BF)
        sends[way, way].start()

    for flip in range(2):
        for d in range(NT):
            if flip == 0 and d == 0:
                continue
            source = 2 * lax.rem(t + d, NT) + (1 - zlo if flip else zlo)
            copy_to(z_out.at[d], z_in.at[source], g3_s.at[d, 0], g3_r.at[source], s, right).wait_recv()
            copy_to(zw_out, zw_in.at[source], zw_s.at[d], zw_r.at[source], s, right).wait_recv()
    parts = [[z_in[k, 0], z_in[k, 1], zw_in[k]] for k in range(2 * NT)]
    summed = [item.astype(F32) for item in parts[0]]
    for part in parts[1:]:
        summed = [value + item.astype(F32) for value, item in zip(summed, part)]
    for p in range(2):
        step_full[core, p, shard] = summed[p] / (summed[2] + damping)

    def g4(step):
        to, device = column(step)
        src = step_full.at[core, :, shard]
        return copy_to(src, src, g4_s.at[to], g4_r.at[q], device, t)

    @pl.loop(1, XY)
    def _(step):
        g4(step).start()

    @pl.loop(1, XY)
    def _(step):
        source = lax.rem(q + step, XY)
        dst = step_full.at[core, :, shard_of(source)]
        copy_to(dst, dst, g4_s.at[source], g4_r.at[source], s, right).wait_recv()

    g5 = copy_to(step_full.at[core], step_full.at[core], g5_s, g5_r, other_core, t)
    g5.start()

    for item in sends.values():
        item.wait_recv()

    def object_rows(rows):
        scale = illum[rows] + damping
        for p in range(2):
            value = total[2, p, rows] + (rs_in[0, p, rows].astype(F32) + rs_in[1, p, rows].astype(F32))
            out_obj[p, rows] = obj[p, rows] + value / scale

    by_rows(object_rows)
    copy_to(step_full.at[1 - core], step_full.at[1 - core], g5_s, g5_r, other_core, t).wait_recv()
    out_probe[...] = step_full[...]

    for item in to_right + to_left + [on_right, on_left, g1w, g5] + forwards + list(sends.values()):
        item.wait_send()
    for d in range(1, NT):
        copy_to(
            modes.at[0, core, :, shard], modes.at[NT - d, core, :, shard],
            pz_s.at[d], pz_r.at[NT - d], s, lax.rem(t + d, NT),
        ).wait_send()
        to_core(d).wait_send()

    for i in range(NT):
        g3(i, 1).wait_send()
        if i > 0:
            g3(i, 0).wait_send()

    @pl.loop(1, 2 * NT)
    def _(k):
        zw(k).wait_send()

    @pl.loop(0, NT)
    def _(i):
        g1(i).wait_send()

    @pl.loop(1, XY)
    def _(step):
        over_columns(step).wait_send()
        g2w(step).wait_send()
        g4(step).wait_send()

        @pl.loop(0, NT)
        def _(i):
            g2(i, step).wait_send()

    @pl.when(has_prev)
    def _():
        for block in (t, left, right, opp):
            for p in range(2):
                passed(block, p).wait_send()

    @pl.when(has_next)
    def _():
        for item in tables:
            item.wait_send()
        for u in range(2):
            pass_sum(u).wait_send()


def shards(NS, NT, object_field, probe_modes, amplitudes, positions, counts):
    W = amplitudes.shape[1]
    XY = NS // 4
    R = W // XY
    fr, fi = dft_tables(W)
    vmem = pl.BlockSpec(memory_space=pltpu.VMEM)
    smem = pl.BlockSpec(memory_space=pltpu.SMEM)
    hbm = pl.BlockSpec(memory_space=pl.ANY)
    dma = pltpu.SemaphoreType.DMA

    def buf(*shape, dtype=F32):
        return pltpu.VMEM(shape, dtype)

    scratch = [
        buf(2, W, W), buf(2, 2, W, W),
        buf(NT, 2, W, W, dtype=BF), buf(NT, 2, W, W, dtype=BF), buf(NT, 2, 2, W, W, dtype=BF),
        buf(2, W, W, dtype=BF), buf(2, W, W), buf(2 * W, 2 * W, dtype=BF), buf(2 * W, 2 * W, dtype=BF),
        buf(2, W, 2 * W, dtype=BF), buf(2 * W, 2 * W, dtype=BF), buf(NT, 2 * W, 2 * W), buf(2 * W, 2 * W),
        buf(W, W), buf(2, W, W), buf(2, 2, W, W), buf(NT, 2, 2, W, W), buf(W, W), buf(W, W), buf(W, W),
        buf(8, 2, dtype=jnp.int32), buf(1, dtype=jnp.int32),
        pltpu.SMEM((8, 2), jnp.int32), pltpu.SMEM((1,), jnp.int32),
        buf(2, 2, W, W, dtype=BF), buf(2, 2, W, W, dtype=BF), buf(3, 2, W, W),
        buf(2, W, W, dtype=BF), buf(2, W, W, dtype=BF), buf(2, 2, W, W, dtype=BF), buf(2, 2, W, W, dtype=BF),
        buf(2 * NT + 1, W, W, dtype=BF), buf(2 * NT + 1, W, W, dtype=BF), buf(2 * NT + 1, W, W, dtype=BF),
        buf(XY, 2 * NT + 1, R, W, dtype=BF), buf(NT, 2, R, W, dtype=BF), buf(R, W, dtype=BF), buf(2 * NT, 2, R, W, dtype=BF), buf(2 * NT, R, W, dtype=BF),
        buf(2, 2, W, W),
        dma((4,)), dma((2,)), dma((2,)), dma((2,)), dma((4,)), dma((4,)), dma((2,)), dma((2,)), dma((4, 2)), dma((4, 2)),
        dma((NT,)), dma((NT,)), dma((XY,)), dma((XY,)), dma((NT,)), dma((NT,)),
        dma((2,)), dma((2,)), dma((2,)), dma((2,)), dma((2, 2)), dma((2, 2)),
        dma((NT + 1,)), dma((NT + 1,)), dma((NT, XY)), dma((NT, XY)), dma((XY,)), dma((XY,)),
        dma((NT, 2)), dma((2 * NT,)), dma((2 * NT,)), dma((2 * NT,)), dma((XY,)), dma((XY,)), dma, dma,
    ]
    new_object, probe_step = pl.pallas_call(
        functools.partial(kernel, W, XY, NS, NT),
        out_shape=(
            jax.ShapeDtypeStruct(object_field.shape, F32),
            jax.ShapeDtypeStruct(probe_modes.shape, F32),
        ),
        in_specs=[hbm, hbm, hbm, smem, smem, vmem, vmem, vmem, vmem],
        out_specs=(vmem, vmem),
        scratch_shapes=scratch,
        compiler_params=pltpu.CompilerParams(
            collective_id=0, has_side_effects=True, vmem_limit_bytes=58 * 1024 * 1024
        ),
    )(object_field, probe_modes, amplitudes, positions, counts, positions, counts, jnp.asarray(fr), jnp.asarray(fi))
    return new_object, probe_step


def solution(mesh):
    placed = (
        P(None, "scan", "tile"),
        P("tile", None, None, None),
        P("scan", None, None),
        P("scan", None),
        P("scan"),
    )
    return jax.shard_map(
        functools.partial(shards, mesh.shape["scan"], mesh.shape["tile"]),
        mesh=mesh,
        in_specs=placed,
        out_specs=(P(None, "scan", "tile"), P("tile", None, None, None)),
        check_vma=False,
    )
```
